128 devices in a mesh: wide: 8 (over y_hi, z), narrow: 16 (over x, y_lo, core).
Axes of the slice: x: 4, y: 4 (y_hi: 2, y_lo: 2; y = y_hi * 2 + y_lo), z: 4, core: 2. Of those that a mesh axis runs over, the one named last changes fastest.
Arguments:
- tokens: bfloat16 [256, 256, 768], P('wide', 'narrow'), may hold values from -6 to 6
- regions: int32 [256, 256], P('wide', 'narrow'), may hold values from 0 to 60
- w_qkv3: bfloat16 [768, 2304], replicated, may hold values from -0.21875 to 0.21875
- w_proj3: bfloat16 [768, 768], replicated, may hold values from -0.21875 to 0.21875
- bias_table3: float32 [24, 31, 31], replicated, may hold values from -3 to 3
- logit_scale3: float32 [24], replicated, may hold values from 2 to 20
- gain_attn3: float32 [768], replicated, may hold values from 0.1 to 1.9
- w_merge: bfloat16 [3072, 1536], replicated, may hold values from -0.109375 to 0.109375
- gain_merge: float32 [1536], replicated, may hold values from 0.1 to 1.9
- w_qkv4: bfloat16 [3, 1536, 1536], P(None, None, 'narrow'), may hold values from -0.15625 to 0.15625
- w_proj4: bfloat16 [1536, 1536], P('narrow'), may hold values from -0.15625 to 0.15625
- bias_table4: float32 [48, 31, 31], P('narrow'), may hold values from -3 to 3
- logit_scale4: float32 [48], P('narrow'), may hold values from 2 to 20
- gain_attn4: float32 [1536], replicated, may hold values from 0.1 to 1.9
- w_up4: bfloat16 [1536, 6144], P(None, 'narrow'), may hold values from -0.15625 to 0.15625
- w_down4: bfloat16 [6144, 1536], P('narrow'), may hold values from -0.078125 to 0.078125
- gain_mlp4: float32 [1536], replicated, may hold values from 0.1 to 1.9
Outputs:
- output: bfloat16 [128, 128, 1536], P('wide', 'narrow')
The draws below stay inside these ranges and needn't reach their ends.
All inputs are finite; a program needn't handle non-finite values.
Results may differ from the reference program's by a relative error of at most 0.033.
Values may be sent and summed in bfloat16 or wider, within the bound.
A program may use at most 256 MiB of HBM per device.

```python
import math
import jax
import jax.numpy as jnp
from jax import lax

C3 = 768
HD = 32
WIN = 16
SHIFT = 8
H3 = 24
C4 = 1536
H4 = 48
MLP4 = 6144
GRID_R = 256
GRID_C = 256


def draw_regions(key, part):
    key = jax.random.fold_in(key, 11)
    key_rows, key_cols = jax.random.split(key)
    cuts_rows = jax.random.randint(key_rows, (3,), SHIFT + 1, GRID_R)
    cuts_cols = jax.random.randint(key_cols, (3,), SHIFT + 1, GRID_C)
    row_pos = (jnp.arange(GRID_R) + SHIFT) % GRID_R
    col_pos = (jnp.arange(GRID_C) + SHIFT) % GRID_C
    band_rows = jnp.sum((row_pos[:, None] >= cuts_rows[None, :]).astype(jnp.int32), 1)
    band_cols = jnp.sum((col_pos[:, None] >= cuts_cols[None, :]).astype(jnp.int32), 1)
    wrap_rows = (jnp.arange(GRID_R) >= GRID_R - SHIFT).astype(jnp.int32)
    wrap_cols = (jnp.arange(GRID_C) >= GRID_C - SHIFT).astype(jnp.int32)
    labels = (band_rows[:, None] * 4 + band_cols[None, :]) * 4 + wrap_rows[:, None] * 2 + wrap_cols[None, :]
    return labels.astype(jnp.int32)


def level_of(own_key, dims, shards, smallest, high):
    def one(axis_at, parts):
        steps = jax.random.uniform(jax.random.fold_in(jax.random.fold_in(own_key, 6), axis_at), (parts,), jnp.float32, smallest / len(shards), high / len(shards))
        return jnp.repeat(jnp.exp(steps), dims[axis_at] // parts).reshape((-1,) + (1,) * (len(dims) - axis_at - 1))

    factor_of = one(*shards[0])
    for cut in shards[1:]:
        factor_of = factor_of * one(*cut)
    return factor_of


def normal_values(stream_key, dims, scale, bound, pieces=(), kind=jnp.bfloat16):
    level = level_of(stream_key, dims, pieces, -0.22, 0.18) if pieces else 1.0
    array = jax.random.normal(stream_key, dims, jnp.float32) * scale * level
    return jnp.minimum(jnp.maximum(array, -bound), bound).astype(kind)


def setup_inputs(seed: int = 0) -> dict:
    key_list = jax.random.split(jax.random.key(seed), 18)
    return {
        "tokens": normal_values(key_list[0], (GRID_R, GRID_C, C3), 1.0, 6.0, ((0, 8), (1, 16))),
        "regions": draw_regions(jax.random.fold_in(key_list[17], 71), 0),
        "w_qkv3": normal_values(key_list[2], (C3, 3 * C3), C3 ** -0.5, 0.21875),
        "w_proj3": normal_values(key_list[3], (C3, C3), C3 ** -0.5, 0.21875),
        "bias_table3": normal_values(key_list[4], (H3, 2 * WIN - 1, 2 * WIN - 1), 0.5, 3.0, (), jnp.float32),
        "logit_scale3": jnp.clip(jnp.exp(jax.random.uniform(key_list[5], (H3,), jnp.float32, math.log(2.0), math.log(20.0))), 2.0, 20.0),
        "gain_attn3": jnp.clip(1.0 + 0.18 * jax.random.normal(key_list[6], (C3,), jnp.float32), 0.1, 1.9),
        "w_merge": normal_values(key_list[7], (4 * C3, C4), (4 * C3) ** -0.5, 0.109375),
        "gain_merge": jnp.clip(1.0 + 0.18 * jax.random.normal(key_list[8], (C4,), jnp.float32), 0.1, 1.9),
        "w_qkv4": normal_values(key_list[9], (3, C4, C4), C4 ** -0.5, 0.15625, ((2, 16),)),
        "w_proj4": normal_values(key_list[10], (C4, C4), C4 ** -0.5, 0.15625, ((0, 16),)),
        "bias_table4": normal_values(key_list[11], (H4, 2 * WIN - 1, 2 * WIN - 1), 0.5, 3.0, ((0, 16),), jnp.float32),
        "logit_scale4": jnp.clip(jnp.exp(math.log(20.0) - 2.3025851 * jax.random.uniform(key_list[12], (H4,), jnp.float32) ** level_of(key_list[12], (H4,), ((0, 16),), -0.2, 0.2)), 2.0, 20.0),
        "gain_attn4": jnp.clip(1.0 + 0.18 * jax.random.normal(key_list[13], (C4,), jnp.float32), 0.1, 1.9),
        "w_up4": normal_values(key_list[14], (C4, MLP4), C4 ** -0.5, 0.15625, ((1, 16),)),
        "w_down4": normal_values(key_list[15], (MLP4, C4), MLP4 ** -0.5, 0.078125, ((0, 16),)),
        "gain_mlp4": jnp.clip(1.0 + 0.18 * jax.random.normal(key_list[16], (C4,), jnp.float32), 0.1, 1.9),
    }


def layer_norm(values, gain):
    center = lax.optimization_barrier(jnp.mean(values, -1, keepdims=True))
    offset = values - center
    spread = lax.optimization_barrier(jnp.mean(offset * offset, -1, keepdims=True))
    return offset * lax.rsqrt(spread + 1e-05) * gain.astype(jnp.float32)

def window_bias(table, window):
    offsets = jnp.arange(window)
    relative = offsets[:, None] - offsets[None, :] + window - 1
    onehot = (relative[:, :, None] == jnp.arange(2 * window - 1)[None, None, :]).astype(jnp.float32)
    values = 16.0 * jax.nn.sigmoid(table.astype(jnp.float32))
    half_rows = jnp.einsum('hpq,acp->hacq', values, onehot, precision=lax.Precision.HIGHEST)
    full_bias = jnp.einsum('hacq,bdq->habcd', half_rows, onehot, precision=lax.Precision.HIGHEST)
    return full_bias.reshape(table.shape[0], window * window, window * window)

def to_windows(field, window):
    row_count, col_count = (field.shape[0], field.shape[1])
    trailing = field.shape[2:]
    blocked = field.reshape((row_count // window, window, col_count // window, window) + trailing)
    blocked = jnp.moveaxis(blocked, 2, 1)
    return blocked.reshape((-1, window * window) + trailing)

def from_windows(blocks, row_count, col_count, window):
    trailing = blocks.shape[2:]
    blocked = blocks.reshape((row_count // window, col_count // window, window, window) + trailing)
    blocked = jnp.moveaxis(blocked, 1, 2)
    return blocked.reshape((row_count, col_count) + trailing)

def attend(qkv_block, scale, bias, key_mask):
    query = qkv_block[:, :, 0].astype(jnp.float32)
    keys = qkv_block[:, :, 1].astype(jnp.float32)
    query = query / jnp.sqrt(lax.optimization_barrier(jnp.sum(query * query, -1, keepdims=True)) + 1e-06)
    keys = keys / jnp.sqrt(lax.optimization_barrier(jnp.sum(keys * keys, -1, keepdims=True)) + 1e-06)
    score = jnp.einsum('nqhd,nkhd->nhqk', query, keys, precision=lax.Precision.HIGHEST)
    score = score * scale.astype(jnp.float32)[None, :, None, None] + bias[None]
    if key_mask is not None:
        score = score + key_mask[:, None]
    expo = jnp.exp(score)
    probs = (expo / lax.optimization_barrier(jnp.sum(expo, -1, keepdims=True))).astype(jnp.bfloat16)
    values = qkv_block[:, :, 2].astype(jnp.float32)
    context = jnp.einsum('nhqk,nkhd->nqhd', probs.astype(jnp.float32), values)
    return context.astype(jnp.bfloat16)

def reference(tokens, regions, w_qkv3, w_proj3, bias_table3, logit_scale3, gain_attn3, w_merge, gain_merge, w_qkv4, w_proj4, bias_table4, logit_scale4, gain_attn4, w_up4, w_down4, gain_mlp4):
    rolled = jnp.roll(tokens, (-SHIFT, -SHIFT), (0, 1))
    qkv_rows = jnp.dot(rolled.reshape(-1, C3), w_qkv3, preferred_element_type=jnp.float32).astype(jnp.bfloat16)
    qkv_wins = to_windows(qkv_rows.reshape(GRID_R, GRID_C, 3, H3, HD), WIN)
    label_wins = to_windows(regions, WIN)
    bias3 = window_bias(bias_table3, WIN)

    def third_window(pair):
        block, label_row = pair
        key_mask = jnp.where(label_row[:, None] == label_row[None, :], 0.0, -100.0).astype(jnp.float32)
        return attend(block[None], logit_scale3, bias3, key_mask[None])[0]
    context = lax.map(third_window, (qkv_wins, label_wins))
    context = from_windows(context, GRID_R, GRID_C, WIN).reshape(-1, C3)
    projected = jnp.dot(context, w_proj3, preferred_element_type=jnp.float32)
    shifted_out = (rolled.reshape(-1, C3).astype(jnp.float32) + layer_norm(projected, gain_attn3)).astype(jnp.bfloat16)
    section_three = jnp.roll(shifted_out.reshape(GRID_R, GRID_C, C3), (SHIFT, SHIFT), (0, 1))
    joined = jnp.concatenate([section_three[0::2, 0::2], section_three[1::2, 0::2], section_three[0::2, 1::2], section_three[1::2, 1::2]], -1)
    merged_rows = jnp.dot(joined.reshape(-1, 4 * C3), w_merge, preferred_element_type=jnp.float32)
    merged = layer_norm(merged_rows, gain_merge).astype(jnp.bfloat16)
    weights_flat = jnp.moveaxis(w_qkv4, 0, 1).reshape(C4, 3 * C4)
    qkv_four = jnp.dot(merged, weights_flat, preferred_element_type=jnp.float32).astype(jnp.bfloat16)
    rows_four = GRID_R // 2
    cols_four = GRID_C // 2
    four_wins = to_windows(qkv_four.reshape(rows_four, cols_four, 3, H4, HD), WIN)
    bias4 = window_bias(bias_table4, WIN)

    def fourth_window(block):
        return attend(block[None], logit_scale4, bias4, None)[0]
    context4 = lax.map(fourth_window, four_wins)
    context4 = from_windows(context4, rows_four, cols_four, WIN).reshape(-1, C4)
    projected4 = jnp.dot(context4, w_proj4, preferred_element_type=jnp.float32)
    hidden = (merged.astype(jnp.float32) + layer_norm(projected4, gain_attn4)).astype(jnp.bfloat16)
    inner_act = jax.nn.gelu(jnp.dot(hidden, w_up4, preferred_element_type=jnp.float32), approximate=False).astype(jnp.bfloat16)
    down_terms = jnp.dot(inner_act, w_down4, preferred_element_type=jnp.float32)
    result = (hidden.astype(jnp.float32) + layer_norm(down_terms, gain_mlp4)).astype(jnp.bfloat16)
    return result.reshape(rows_four, cols_four, C4)
```

```python
import functools
import math

import jax
import jax.numpy as jnp
from jax import lax
from jax.experimental import pallas as pl
from jax.experimental.pallas import tpu as pltpu
from jax.sharding import PartitionSpec as P

HD = 32
LOG2E = math.log2(math.e)
MESH = pl.DeviceIdType.MESH
BF = jnp.bfloat16
F32 = jnp.float32
MASK_HI = 144.0
MASK_LO = 100.0 * LOG2E - 144.0
VMEM_LIMIT = 60 << 20


def place():
    wide, narrow = lax.axis_index("wide"), lax.axis_index("narrow")
    return wide, narrow


def shifted(dw, dn):
    wide, narrow = place()
    return (lax.rem(wide + dw + 8, 8), lax.rem(narrow + dn + 16, 16))


def along_x(step):
    wide, narrow = place()
    return (wide, lax.rem(narrow + 4 * step + 16, 16))


def along_y(step):
    wide, narrow = place()
    y = (wide // 4) * 2 + lax.rem(narrow // 2, 2)
    y = lax.rem(y + step + 4, 4)
    return (
        (y // 2) * 4 + lax.rem(wide, 4),
        (narrow // 4) * 4 + lax.rem(y, 2) * 2 + lax.rem(narrow, 2),
    )


def other_core():
    wide, narrow = place()
    return (wide, narrow + 1 - 2 * lax.rem(narrow, 2))


def quad(core, row):
    wide, narrow = place()
    c, r = lax.rem(narrow, 2), lax.rem(narrow // 2, 2)
    c = 1 - c if core else c
    r = 1 - r if row else r
    return (wide, (narrow // 4) * 4 + r * 2 + c)


def greet(sources, expected):
    barrier = pltpu.get_barrier_semaphore()
    for device in sources:
        pl.semaphore_signal(barrier, inc=1, device_id=device, device_id_type=MESH)
    pl.semaphore_wait(barrier, expected)


class Wires:
    def __init__(self, send, recv):
        self.send, self.recv, self.count = send, recv, 0

    def copy(self, src, dst, device):
        i = self.count
        self.count += 1
        out = pltpu.make_async_remote_copy(
            src_ref=src,
            dst_ref=dst,
            send_sem=self.send.at[i],
            recv_sem=self.recv.at[i],
            device_id=device,
            device_id_type=MESH,
        )
        return out

    def go(self, src, dst, device):
        out = self.copy(src, dst, device)
        out.start()
        return out


def dot(a, b):
    return jnp.dot(a, b, preferred_element_type=F32)


def dot_nt(a, b):
    return lax.dot_general(a, b, (((1,), (1,)), ((), ())), preferred_element_type=F32)


def layer_norm(values, gain):
    center = jnp.mean(values, -1, keepdims=True)
    offset = values - center
    spread = jnp.mean(offset * offset, -1, keepdims=True)
    return offset * lax.rsqrt(spread + 1e-05) * gain


def lane_mask(head, last=False):
    lane = lax.broadcasted_iota(jnp.int32, (1, 128), 1)
    keep = lane >= head * HD
    if not last:
        keep = keep & (lane < (head + 1) * HD)
    return jnp.where(keep, 1.0, 0.0)


def head_ones():
    row = lax.rem(lax.broadcasted_iota(jnp.int32, (256, 128), 0), 128) // HD
    col = lax.broadcasted_iota(jnp.int32, (256, 128), 1) // HD
    return jnp.where(row == col, 1.0, 0.0).astype(BF)


def squares_by_head(values, ones):
    square = values * values
    high = square.astype(BF)
    low = (square - high.astype(F32)).astype(BF)
    return dot(jnp.concatenate([high, low], 1), ones)


def bias_tables(rows):
    sub = lax.broadcasted_iota(jnp.int32, (8, 256), 0)
    lane = lax.rem(lax.broadcasted_iota(jnp.int32, (8, 256), 1), 8)
    spread = [jnp.broadcast_to(rows[m : m + 1], (8, 256)) for m in range(4)]
    tables = []
    for m in range(1, 4):
        straight = pltpu.roll(spread[m], 0, 1, stride=1, stride_axis=0)
        around = pltpu.roll(spread[m - 1], 248, 1, stride=1, stride_axis=0)
        tables.append(jnp.where(lane >= sub, straight, around))
    return tables


def bias_block(table, a):
    return pltpu.roll(table, (256 - 8 * (15 - a)) % 256, 1)[:, :128]


def halo_kernel(t_ref, q_ref, r_ref, g_ref, send, recv, local):
    greet(
        [shifted(1, 0), shifted(0, 1), shifted(1, 1), quad(1, 0), quad(0, 1), quad(1, 1)], 6
    )
    w = Wires(send, recv)
    inner = pltpu.make_async_copy(
        t_ref.at[1, pl.ds(64, 192)], r_ref.at[0, pl.ds(0, 192)], local.at[0]
    )
    cps = [
        w.go(t_ref.at[0, pl.ds(64, 192)], r_ref.at[1, pl.ds(0, 192)], shifted(0, -1)),
        w.go(t_ref.at[1, pl.ds(0, 64)], r_ref.at[0, pl.ds(192, 64)], shifted(-1, 0)),
        w.go(t_ref.at[0, pl.ds(0, 64)], r_ref.at[1, pl.ds(192, 64)], shifted(-1, -1)),
    ]
    inner.start()
    cps += [
        w.go(q_ref, g_ref.at[0], quad(1, 0)),
        w.go(q_ref, g_ref.at[1], quad(0, 1)),
        w.go(q_ref, g_ref.at[2], quad(1, 1)),
    ]
    inner.wait()
    for c in cps:
        c.wait()


def halo(tokens, table4):
    any_ = pl.BlockSpec(memory_space=pl.ANY)
    return pl.pallas_call(
        halo_kernel,
        name="halo",
        out_shape=(
            jax.ShapeDtypeStruct((2, 256, 768), BF),
            jax.ShapeDtypeStruct((3, 3, 8, 256), F32),
        ),
        in_specs=[any_, any_],
        out_specs=(any_, any_),
        scratch_shapes=[
            pltpu.SemaphoreType.DMA((6,)),
            pltpu.SemaphoreType.DMA((6,)),
            pltpu.SemaphoreType.DMA((1,)),
        ],
        compiler_params=pltpu.CompilerParams(collective_id=1, has_side_effects=True),
    )(tokens, table4)


def third_kernel(
    x_ref,
    aug_ref,
    tab_ref,
    scale_ref,
    wqkv_ref,
    wproj_ref,
    gain_ref,
    wm_hbm,
    gm_ref,
    o_ref,
    qkv,
    ctx,
    bias,
    flat,
    wm,
    mg,
    sem,
):
    fetch = pltpu.make_async_copy(wm_hbm, wm, sem)
    fetch.start()
    x = x_ref[...].reshape(512, 768)

    def project(n, carry):
        cols = pl.ds(pl.multiple_of(n * 256, 256), 256)
        out = dot(x, wqkv_ref[:, cols]).astype(BF)
        qkv[2 * n] = out[:, :128]
        qkv[2 * n + 1] = out[:, 128:]
        return carry

    lax.fori_loop(0, 9, project, 0)

    ones = head_ones()
    masks = [lane_mask(h).astype(BF) for h in range(4)]
    lane = lax.broadcasted_iota(jnp.int32, (1, 128), 1)
    level = jnp.where(
        lane < 61,
        MASK_HI,
        jnp.where(lane < 64, -MASK_HI, jnp.where(lane < 125, MASK_LO, -MASK_LO)),
    ).astype(BF)

    def group(g, carry):
        for h in range(4):
            tables = bias_tables(tab_ref[4 * g + h])
            for t in range(3):
                for a in range(16):
                    bias[h, t, pl.ds(8 * a, 8), :] = bias_block(tables[t], a)
        scale = scale_ref[g]
        for w in range(2):

            def rows(j):
                return jnp.concatenate(
                    [
                        qkv[6 * j + g, pl.ds(128 * w, 128), :],
                        qkv[6 * j + g, pl.ds(256 + 128 * w, 128), :],
                    ],
                    0,
                )

            q, k, v = rows(0).astype(F32), rows(1).astype(F32), rows(2)
            aug = jnp.concatenate(
                [aug_ref[pl.ds(128 * w, 128), :], aug_ref[pl.ds(256 + 128 * w, 128), :]], 0
            )
            qn = (q * (lax.rsqrt(squares_by_head(q, ones) + 1e-06) * scale)).astype(BF)
            kn = (k * lax.rsqrt(squares_by_head(k, ones) + 1e-06)).astype(BF)
            keys = jnp.concatenate([kn, aug], 1)
            qaug = aug * level
            acc = jnp.zeros((256, 256), F32)
            for h in range(4):
                score = dot_nt(jnp.concatenate([qn * masks[h], qaug], 1), keys)
                middle = bias[h, 1]
                spot = jnp.concatenate(
                    [
                        jnp.concatenate([middle, bias[h, 2]], 1),
                        jnp.concatenate([bias[h, 0], middle], 1),
                    ],
                    0,
                )
                expo = jnp.exp2(score + spot).astype(BF)
                right = jnp.concatenate(
                    [v * masks[h], jnp.broadcast_to(masks[h], (256, 128))], 1
                )
                acc = acc + dot(expo, right)
            out = (acc[:, :128] / acc[:, 128:]).astype(BF)
            cols = pl.ds(pl.multiple_of(g * 128, 128), 128)
            ctx[pl.ds(128 * w, 128), cols] = out[:128]
            ctx[pl.ds(256 + 128 * w, 128), cols] = out[128:]
        return carry

    lax.fori_loop(0, 6, group, 0)

    for half in range(2):
        for part in range(2):
            start = half * 256 + part * 128
            y = dot(ctx[pl.ds(start, 128), :], wproj_ref[...])
            y = layer_norm(y, gain_ref[...]) + x_ref[half, pl.ds(part * 128, 128), :].astype(F32)
            y = y.astype(BF).astype(F32)
            for r in range(16):
                for m in range(6):
                    flat[m, pl.ds((part * 16 + r) * 16 + half * 8, 8), :] = y[
                        8 * r : 8 * r + 8, 128 * m : 128 * m + 128
                    ]

    fetch.wait()
    pieces = []
    for j in range(2):
        side = jnp.concatenate(
            [flat[m, pl.ds(j, 256, stride=2), :] for m in range(6)], 1
        ).reshape(16, 2, 8, 768)
        for i in range(2):
            pieces.append(side[:, i].reshape(128, 768).astype(BF))
    joined = jnp.concatenate(pieces, 1)

    def merge(n, carry):
        cols = pl.ds(pl.multiple_of(n * 256, 256), 256)
        mg[:, cols] = dot(joined, wm[:, cols])
        return carry

    lax.fori_loop(0, 6, merge, 0)
    merged = layer_norm(mg[...], gm_ref[...]).astype(BF)
    row = lax.broadcasted_iota(jnp.int32, (128, 128), 0)
    col = lax.broadcasted_iota(jnp.int32, (128, 128), 1)
    source = lax.rem(row, 64) // 4 * 8 + row // 64 * 4 + lax.rem(row, 4)
    order = jnp.where(col == source, 1.0, 0.0).astype(BF)
    o_ref[...] = dot(order, merged).astype(BF).reshape(2, 64, 1536)


def third(x, aug, tab, scale, wqkv, wproj, gain, wm, gm):
    vm = pl.BlockSpec(memory_space=pltpu.VMEM)
    return pl.pallas_call(
        third_kernel,
        name="third",
        out_shape=jax.ShapeDtypeStruct((2, 64, 1536), BF),
        in_specs=[vm] * 7 + [pl.BlockSpec(memory_space=pl.ANY), vm],
        out_specs=vm,
        scratch_shapes=[
            pltpu.VMEM((18, 512, 128), BF),
            pltpu.VMEM((512, 768), BF),
            pltpu.VMEM((4, 3, 128, 128), F32),
            pltpu.VMEM((6, 512, 128), F32),
            pltpu.VMEM((3072, 1536), BF),
            pltpu.VMEM((128, 1536), F32),
            pltpu.SemaphoreType.DMA,
        ],
        compiler_params=pltpu.CompilerParams(vmem_limit_bytes=VMEM_LIMIT),
        cost_estimate=pl.CostEstimate(
            flops=5_000_000_000, bytes_accessed=16_000_000, transcendentals=3_200_000
        ),
    )(x, aug, tab, scale, wqkv, wproj, gain, wm, gm)


def start_weights(w, weights, gathered):
    flight = []
    for own, (oc, yy, yc) in zip(weights, gathered):
        half = own.shape[0] // 2
        first, second = pl.ds(0, half), pl.ds(half, half)
        a = w.go(own.at[first], yy.at[first], along_y(1))
        b = w.go(own.at[second], yy.at[second], along_y(-1))
        c = w.go(own, oc, other_core())
        flight.append((a, b, c, yy, yc, first, second))
    return flight


def finish_weights(w, flight):
    late = []
    for a, b, c, yy, yc, first, second in flight:
        a.wait_recv()
        late.append(w.go(yy.at[first], yc.at[first], other_core()))
        b.wait_recv()
        late.append(w.go(yy.at[second], yc.at[second], other_core()))
    for a, b, c, *_ in flight:
        a.wait_send()
        b.wait_send()
        c.wait()
    for c in late:
        c.wait()


def gathered_shapes(shapes):
    return tuple(jax.ShapeDtypeStruct(s, BF) for s in shapes for _ in range(3))


def ring_gather(w, blocks):
    right = w.go(blocks.at[0], blocks.at[1], along_x(1))
    left = w.go(blocks.at[0], blocks.at[2], along_x(-1))
    first, second = pl.ds(0, 64), pl.ds(64, 64)
    right.wait_recv()
    on_right = w.go(blocks.at[1, first], blocks.at[3, first], along_x(1))
    yield 1
    left.wait_recv()
    on_left = w.go(blocks.at[2, second], blocks.at[3, second], along_x(-1))
    yield 2
    on_right.wait_recv()
    on_left.wait_recv()
    yield 3
    for c in (right, left, on_right, on_left):
        c.wait_send()


def spread_kernel(m_ref, wa_ref, wp_ref, t_ref, o_ref, *rest):
    gathered, (send, recv, local) = rest[:6], rest[6:]
    greet(
        [
            shifted(0, -1),
            shifted(-1, 0),
            shifted(-1, -1),
            along_x(1),
            along_x(-1),
            along_y(1),
            along_y(-1),
            other_core(),
        ],
        8,
    )
    w = Wires(send, recv)
    inner = pltpu.make_async_copy(
        m_ref.at[0, pl.ds(0, 48)], t_ref.at[0, pl.ds(80, 48)], local.at[0]
    )
    cps = [
        w.go(m_ref.at[1, pl.ds(0, 48)], t_ref.at[0, pl.ds(16, 48)], shifted(0, 1)),
        w.go(m_ref.at[0, pl.ds(48, 16)], t_ref.at[0, pl.ds(64, 16)], shifted(1, 0)),
        w.go(m_ref.at[1, pl.ds(48, 16)], t_ref.at[0, pl.ds(0, 16)], shifted(1, 1)),
    ]
    inner.start()
    flight = start_weights(w, (wa_ref, wp_ref), (gathered[:3], gathered[3:]))
    inner.wait()
    for c in cps:
        c.wait_recv()
    core = [w.copy(t_ref.at[b], o_ref.at[b], other_core()) for b in range(4)]
    core[0].start()
    for b in ring_gather(w, t_ref):
        core[b].start()
    finish_weights(w, flight)
    for c in core:
        c.wait()
    for c in cps:
        c.wait_send()


def spread(merged, wa, wp):
    any_ = pl.BlockSpec(memory_space=pl.ANY)
    n = 3 + 6 + 4 + 4 + 4
    return pl.pallas_call(
        spread_kernel,
        name="spread",
        out_shape=(
            jax.ShapeDtypeStruct((4, 128, 1536), BF),
            jax.ShapeDtypeStruct((4, 128, 1536), BF),
        )
        + gathered_shapes([wa.shape, wp.shape]),
        in_specs=[any_] * 3,
        out_specs=(any_,) * 8,
        scratch_shapes=[
            pltpu.SemaphoreType.DMA((n,)),
            pltpu.SemaphoreType.DMA((n,)),
            pltpu.SemaphoreType.DMA((1,)),
        ],
        compiler_params=pltpu.CompilerParams(collective_id=2, has_side_effects=True),
    )(merged, wa, wp)


def fourth_kernel(
    t_ref, o_ref, tab_ref, w0, w1, w2, w3, p0, p1, p2, p3, part_ref, own_ref, bias, wp, qkv
):
    core = lax.rem(lax.axis_index("narrow"), 2)
    for s, p in enumerate((p0, p1, p2, p3)):
        wp[pl.ds(128 * s, 96), :] = p[...]
        wp[pl.ds(128 * s + 96, 32), :] = jnp.zeros((32, 1536), BF)

    def build(n, carry):
        rows = tab_ref[n]
        tables = bias_tables(rows)
        side = jnp.where(core == 0, tables[2], tables[0])
        for a in range(16):
            bias[n, pl.ds(8 * a, 8), pl.ds(0, 128)] = bias_block(tables[1], a)
            bias[n, pl.ds(8 * a, 8), pl.ds(128, 128)] = bias_block(side, a)
        return carry

    lax.fori_loop(0, 12, build, 0)
    ones = head_ones()
    masks = [lane_mask(h, h == 2).astype(BF) for h in range(3)]
    row = lax.broadcasted_iota(jnp.int32, (128, 128), 0)
    col = lax.broadcasted_iota(jnp.int32, (128, 128), 1)
    source = lax.rem(row, 8) // 4 * 64 + row // 8 * 4 + lax.rem(row, 4)
    order = jnp.where(col == source, 1.0, 0.0).astype(BF)

    def block(b, carry):
        mine = dot(order, t_ref[b]).astype(BF)
        theirs = dot(order, o_ref[b]).astype(BF)

        @pl.when(b == 0)
        def _():
            own_ref[...] = mine

        both = jnp.concatenate([mine, theirs], 0)
        outs = []
        for s, wa in enumerate((w0, w1, w2, w3)):
            qkv[...] = dot(both, wa[...]).astype(BF)
            q = qkv[pl.ds(0, 128), pl.ds(0, 128)].astype(F32)
            k = qkv[:, pl.ds(128, 128)].astype(F32)
            v = qkv[:, pl.ds(256, 128)]
            scale = tab_ref[3 * s, 5:6, :128]
            qn = (q * (lax.rsqrt(squares_by_head(q, ones) + 1e-06) * scale)).astype(BF)
            kn = (k * lax.rsqrt(squares_by_head(k, ones) + 1e-06)).astype(BF)
            acc = jnp.zeros((128, 256), F32)
            for h in range(3):
                score = dot_nt(qn * masks[h], kn)
                expo = jnp.exp2(score + bias[3 * s + h]).astype(BF)
                right = jnp.concatenate(
                    [v * masks[h], jnp.broadcast_to(masks[h], (256, 128))], 1
                )
                acc = acc + dot(expo, right)
            outs.append((acc[:, :128] / acc[:, 128:]).astype(BF))
        part_ref[b] = dot(jnp.concatenate(outs, 1), wp[...]).astype(BF)
        return carry

    lax.fori_loop(0, 4, block, 0)


def fourth(t, o, tab, was, wps):
    vm = pl.BlockSpec(memory_space=pltpu.VMEM)
    return pl.pallas_call(
        fourth_kernel,
        name="fourth",
        out_shape=(
            jax.ShapeDtypeStruct((4, 128, 1536), BF),
            jax.ShapeDtypeStruct((128, 1536), BF),
        ),
        in_specs=[vm] * 11,
        out_specs=(vm, vm),
        scratch_shapes=[
            pltpu.VMEM((12, 128, 256), F32),
            pltpu.VMEM((512, 1536), BF),
            pltpu.VMEM((256, 384), BF),
        ],
        compiler_params=pltpu.CompilerParams(vmem_limit_bytes=VMEM_LIMIT),
    )(t, o, tab, *was, *wps)


def ring_sum(w, part, buf):
    first, second = pl.ds(0, 64), pl.ds(64, 64)
    far_right = w.go(part.at[3, first], buf.at[0], along_x(1))
    far_left = w.go(part.at[3, second], buf.at[1], along_x(-1))
    near_right = w.go(part.at[2, second], buf.at[2], along_x(1))
    near_left = w.go(part.at[1, first], buf.at[3], along_x(-1))
    far_right.wait_recv()
    part[2, first, :] = (part[2, first, :].astype(F32) + buf[0].astype(F32)).astype(BF)
    last_right = w.go(part.at[2, first], buf.at[4], along_x(1))
    far_left.wait_recv()
    part[1, second, :] = (part[1, second, :].astype(F32) + buf[1].astype(F32)).astype(BF)
    last_left = w.go(part.at[1, second], buf.at[5], along_x(-1))
    near_right.wait_recv()
    near_left.wait_recv()
    last_right.wait_recv()
    last_left.wait_recv()
    top = part[0, first, :].astype(F32) + buf[4].astype(F32) + buf[3].astype(F32)
    low = part[0, second, :].astype(F32) + buf[2].astype(F32) + buf[5].astype(F32)
    for c in (far_right, far_left, near_right, near_left, last_right, last_left):
        c.wait_send()
    return jnp.concatenate([top, low], 0)


def middle_kernel(p_ref, own_ref, gain_ref, wu_ref, wd_ref, h_ref, *rest):
    gathered, (part, buf, send, recv, local) = rest[:6], rest[6:]
    greet([along_x(1), along_x(-1), along_y(1), along_y(-1), other_core()], 5)
    w = Wires(send, recv)
    take = pltpu.make_async_copy(p_ref, part, local.at[0])
    take.start()
    flight = start_weights(w, (wu_ref, wd_ref), (gathered[:3], gathered[3:]))
    take.wait()
    total = ring_sum(w, part, buf)
    h_ref[0] = (own_ref[...].astype(F32) + layer_norm(total, gain_ref[...])).astype(BF)
    for _ in ring_gather(w, h_ref):
        pass
    finish_weights(w, flight)


def middle(part, own, gain, wu, wd):
    any_ = pl.BlockSpec(memory_space=pl.ANY)
    vm = pl.BlockSpec(memory_space=pltpu.VMEM)
    n = 6 + 6 + 4 + 4
    return pl.pallas_call(
        middle_kernel,
        name="middle",
        out_shape=(jax.ShapeDtypeStruct((4, 128, 1536), BF),)
        + gathered_shapes([wu.shape, wd.shape]),
        in_specs=[any_, vm, vm, any_, any_],
        out_specs=(vm,) + (any_,) * 6,
        scratch_shapes=[
            pltpu.VMEM((4, 128, 1536), BF),
            pltpu.VMEM((6, 64, 1536), BF),
            pltpu.SemaphoreType.DMA((n,)),
            pltpu.SemaphoreType.DMA((n,)),
            pltpu.SemaphoreType.DMA((1,)),
        ],
        compiler_params=pltpu.CompilerParams(
            collective_id=3, has_side_effects=True, vmem_limit_bytes=VMEM_LIMIT
        ),
    )(part, own, gain, wu, wd)


def last_kernel(p_ref, h_ref, gain_ref, out_ref, part, buf, send, recv, local):
    greet([along_x(1), along_x(-1)], 2)
    w = Wires(send, recv)
    take = pltpu.make_async_copy(p_ref, part, local.at[0])
    take.start()
    take.wait()
    total = ring_sum(w, part, buf)
    out_ref[...] = (h_ref[0].astype(F32) + layer_norm(total, gain_ref[...])).astype(BF)


def last(part, hidden, gain):
    any_ = pl.BlockSpec(memory_space=pl.ANY)
    vm = pl.BlockSpec(memory_space=pltpu.VMEM)
    return pl.pallas_call(
        last_kernel,
        name="last",
        out_shape=jax.ShapeDtypeStruct((128, 1536), BF),
        in_specs=[any_, vm, vm],
        out_specs=vm,
        scratch_shapes=[
            pltpu.VMEM((4, 128, 1536), BF),
            pltpu.VMEM((6, 64, 1536), BF),
            pltpu.SemaphoreType.DMA((6,)),
            pltpu.SemaphoreType.DMA((6,)),
            pltpu.SemaphoreType.DMA((1,)),
        ],
        compiler_params=pltpu.CompilerParams(
            collective_id=4, has_side_effects=True, vmem_limit_bytes=VMEM_LIMIT
        ),
    )(part, hidden, gain)


def gelu(x):
    return 0.5 * x * (1.0 + lax.erf(x * (2.0**-0.5)))


def mlp_kernel(h_ref, u0, u1, u2, u3, d0, d1, d2, d3, part_ref, acc):
    h = h_ref[...].reshape(512, 1536)
    for s, (wu, wd) in enumerate(((u0, d0), (u1, d1), (u2, d2), (u3, d3))):
        inner = gelu(dot(h, wu[...])).astype(BF)

        def down(n, carry):
            cols = pl.ds(pl.multiple_of(n * 256, 256), 256)
            term = dot(inner, wd[:, cols])
            if s > 0:
                term = term + acc[:, cols]
            if s < 3:
                acc[:, cols] = term
            else:
                part_ref[:, :, cols] = term.astype(BF).reshape(4, 128, 256)
            return carry

        lax.fori_loop(0, 6, down, 0)


def mlp(hidden, wus, wds):
    vm = pl.BlockSpec(memory_space=pltpu.VMEM)
    return pl.pallas_call(
        mlp_kernel,
        name="mlp",
        out_shape=jax.ShapeDtypeStruct((4, 128, 1536), BF),
        in_specs=[vm] * 9,
        out_specs=vm,
        scratch_shapes=[pltpu.VMEM((512, 1536), F32)],
        compiler_params=pltpu.CompilerParams(vmem_limit_bytes=VMEM_LIMIT),
    )(hidden, *wus, *wds)


def table_rows(table):
    heads = table.shape[0]
    values = 16.0 * LOG2E * jax.nn.sigmoid(table[:, ::-1, ::-1])
    values = jnp.pad(values, ((0, 0), (0, 1), (1, 0)))
    values = values.reshape(heads, 32, 4, 8).transpose(0, 2, 1, 3).reshape(heads, 4, 256)
    return jnp.pad(values, ((0, 0), (0, 4), (0, 0)))


def per_device(
    tokens,
    regions,
    w_qkv3,
    w_proj3,
    bias_table3,
    logit_scale3,
    gain_attn3,
    w_merge,
    gain_merge,
    w_qkv4,
    w_proj4,
    bias_table4,
    logit_scale4,
    gain_attn4,
    w_up4,
    w_down4,
    gain_mlp4,
):
    halves = tokens.reshape(32, 2, 8, 768).transpose(1, 0, 2, 3).reshape(2, 256, 768)
    tab4 = table_rows(bias_table4)
    scale4 = jnp.pad(jnp.repeat(logit_scale4 * LOG2E, HD), (0, 160))
    tab4 = tab4.at[0, 5].set(scale4)
    rolled, tabs = halo(halves, tab4)

    labels = regions.reshape(32, 2, 8).transpose(1, 0, 2).reshape(512, 1)
    lane = jnp.arange(128)[None, :]
    aug = (labels == lane) | (labels + 64 == lane) | (lane == 61) | (lane == 125)
    scale3 = jnp.repeat(logit_scale3 * LOG2E, HD).reshape(6, 1, 128)
    merged = third(
        rolled,
        aug.astype(BF),
        table_rows(bias_table3),
        scale3,
        w_qkv3,
        w_proj3,
        gain_attn3[None],
        w_merge,
        gain_merge[None],
    )
    wa = jnp.pad(w_qkv4, ((0, 0), (0, 0), (0, 32))).transpose(1, 0, 2).reshape(1536, 384)
    t, o, *gathered = spread(merged, wa, w_proj4)
    tab_all = jnp.concatenate([tab4[None], tabs], 0).reshape(12, 8, 256)
    part, own = fourth(t, o, tab_all, [wa] + gathered[:3], [w_proj4] + gathered[3:])
    hidden, *gathered = middle(part, own, gain_attn4[None], w_up4, w_down4)
    part = mlp(hidden, [w_up4] + gathered[:3], [w_down4] + gathered[3:])
    out = last(part, hidden, gain_mlp4[None])
    return out.reshape(16, 8, 1536)


def solution(mesh):
    placed = (
        P("wide", "narrow", None),
        P("wide", "narrow"),
        P(),
        P(),
        P(),
        P(),
        P(),
        P(),
        P(),
        P(None, None, "narrow"),
        P("narrow", None),
        P("narrow", None, None),
        P("narrow"),
        P(),
        P(None, "narrow"),
        P("narrow", None),
        P(),
    )
    return jax.shard_map(
        per_device, mesh=mesh, in_specs=placed, out_specs=P("wide", "narrow", None), check_vma=False
    )
```

```python
import jax
import jax.numpy as jnp
from jax import lax
from jax.experimental import pallas as pl
from jax.experimental.pallas import tpu as pltpu
from jax.sharding import PartitionSpec as P

HD = 32
MESH = pl.DeviceIdType.MESH
BF = jnp.bfloat16
F32 = jnp.float32
MASK = 100.0
WIRES = 64
VMEM_LIMIT = 60 << 20


def place():
    wide, narrow = lax.axis_index("wide"), lax.axis_index("narrow")
    return wide, narrow


def shifted(dw, dn):
    wide, narrow = place()
    return (lax.rem(wide + dw + 8, 8), lax.rem(narrow + dn + 16, 16))


def along_x(step):
    wide, narrow = place()
    return (wide, lax.rem(narrow + 4 * step + 16, 16))


def along_y(step):
    wide, narrow = place()
    y = (wide // 4) * 2 + lax.rem(narrow // 2, 2)
    y = lax.rem(y + step + 4, 4)
    return (
        (y // 2) * 4 + lax.rem(wide, 4),
        (narrow // 4) * 4 + lax.rem(y, 2) * 2 + lax.rem(narrow, 2),
    )


def other_core():
    wide, narrow = place()
    return (wide, narrow + 1 - 2 * lax.rem(narrow, 2))


def quad(core, row):
    wide, narrow = place()
    c, r = lax.rem(narrow, 2), lax.rem(narrow // 2, 2)
    c = 1 - c if core else c
    r = 1 - r if row else r
    return (wide, (narrow // 4) * 4 + r * 2 + c)


def greet(sources, expected):
    barrier = pltpu.get_barrier_semaphore()
    for device in sources:
        pl.semaphore_signal(barrier, inc=1, device_id=device, device_id_type=MESH)
    pl.semaphore_wait(barrier, expected)


class Wires:
    def __init__(self, send, recv):
        self.send, self.recv, self.count = send, recv, 0

    def copy(self, src, dst, device):
        i = self.count
        self.count += 1
        out = pltpu.make_async_remote_copy(
            src_ref=src,
            dst_ref=dst,
            send_sem=self.send.at[i],
            recv_sem=self.recv.at[i],
            device_id=device,
            device_id_type=MESH,
        )
        return out

    def go(self, src, dst, device):
        out = self.copy(src, dst, device)
        out.start()
        return out


def dot(a, b):
    return jnp.dot(a, b, preferred_element_type=F32)


def dot_nt(a, b):
    return lax.dot_general(a, b, (((1,), (1,)), ((), ())), preferred_element_type=F32)


def iota(shape, axis):
    return lax.broadcasted_iota(jnp.int32, shape, axis)


def layer_norm(values, gain):
    center = jnp.mean(values, -1, keepdims=True)
    offset = values - center
    spread = jnp.mean(offset * offset, -1, keepdims=True)
    return offset * lax.rsqrt(spread + 1e-05) * gain


def gelu(x):
    return 0.5 * x * (1.0 + lax.erf(x * (2.0**-0.5)))


def head_blocks():
    same = iota((256, 256), 0) // HD == iota((256, 256), 1) // HD
    return jnp.where(same, 1.0, 0.0).astype(BF)


def inverse_norms(values, blocks):
    return lax.rsqrt(dot((values * values).astype(BF), blocks) + 1e-06)


def lane_pick(values):
    lane = iota((1, 128), 1)
    out = values[0]
    for h in range(1, len(values)):
        out = jnp.where(lane >= h * HD, values[h], out)
    return out


def head_masks(count):
    lane = iota((1, 128), 1) // HD
    return [jnp.where(lane == h, 1.0, 0.0).astype(BF) for h in range(count)]


def table_rows(tables):
    lane = iota((256, 1024), 1)
    spot = lax.rem(iota((256, 1024), 0), 128)
    pick = jnp.where(spot == 31 - 8 * (lane // 256) - lax.rem(lane, 8), 1.0, 0.0).astype(BF)
    high = tables.astype(BF)
    low = (tables - high.astype(F32)).astype(BF)
    moved = dot(jnp.concatenate([high, low], 1), pick)
    row = lax.rem(iota(moved.shape, 0), 32)
    f = lax.rem(iota(moved.shape, 1), 256) // 8
    return jnp.where(row == 30 - f, moved, 0.0)


def head_row(moved, head):
    values = jnp.sum(moved[32 * head : 32 * head + 32], 0, keepdims=True)
    return 16.0 / (1.0 + jnp.exp(-values))


def bias_tables(rows):
    sub = iota((8, 256), 0)
    lane = lax.rem(iota((8, 256), 1), 8)
    spread = [jnp.broadcast_to(r, (8, 256)) for r in rows]
    tables = []
    for m in range(1, 4):
        straight = pltpu.roll(spread[m], 0, 1, stride=1, stride_axis=0)
        around = pltpu.roll(spread[m - 1], 248, 1, stride=1, stride_axis=0)
        tables.append(jnp.where(lane >= sub, straight, around))
    return tables


def bias_block(table, a):
    return pltpu.roll(table, (256 - 8 * (15 - a)) % 256, 1)[:, :128]


def whole_kernel(
    tokens_ref,
    small_ref,
    scale3_ref,
    scale4_ref,
    wqkv3_hbm,
    wproj3_hbm,
    gain_attn3,
    wm_hbm,
    gain_merge,
    wqkv4_hbm,
    wproj4_hbm,
    gain_attn4,
    wup_hbm,
    wdown_hbm,
    gain_mlp4,
    out_ref,
    ctx,
    xs,
    xr,
    aug,
    wqkv,
    wproj,
    wm,
    qkv,
    bias3,
    flat,
    m4,
    back,
    tabs,
    bias4,
    wtmp,
    wa,
    wp,
    blocks,
    others,
    qkv4,
    part,
    buf4,
    bufm,
    hidden,
    wu,
    wd,
    send,
    recv,
    local,
):
    w = Wires(send, recv)
    core = lax.rem(lax.axis_index("narrow"), 2)
    first, second = pl.ds(0, 64), pl.ds(64, 64)

    loads = []
    for i, (src, dst) in enumerate(
        (
            (tokens_ref, ctx),
            (wqkv4_hbm, wtmp),
            (wproj4_hbm, wp.at[0, pl.ds(0, 96)]),
            (wqkv3_hbm, wqkv),
            (wproj3_hbm, wproj),
            (wm_hbm, wm),
            (wup_hbm, wu.at[:, pl.ds(0, 384)]),
            (wdown_hbm, wd.at[pl.ds(0, 384)]),
        )
    ):
        load = pltpu.make_async_copy(src, dst, local.at[i])
        load.start()
        loads.append(load)
    get_tokens, get_qkv4, get_proj4, get_qkv3, get_proj3, get_merge, get_up, get_down = loads

    partners = [shifted(i, j) for i, j in ((0, 1), (1, 0), (1, 1), (0, -1), (-1, 0), (-1, -1))]
    partners += [quad(1, 0), quad(0, 1), quad(1, 1), along_x(1), along_x(-1), along_x(2)]
    partners += [along_y(1), along_y(-1)]
    greet(partners, len(partners))

    get_tokens.wait()
    grouped = ctx[...].astype(F32).reshape(32, 2, 8, 768)
    for half in range(2):
        xs[half] = grouped[:, half].reshape(256, 768).astype(BF)
    halo = [
        w.go(xs.at[0, pl.ds(64, 192)], xr.at[1, pl.ds(0, 192)], shifted(0, -1)),
        w.go(xs.at[1, pl.ds(0, 64)], xr.at[0, pl.ds(192, 64)], shifted(-1, 0)),
        w.go(xs.at[0, pl.ds(0, 64)], xr.at[1, pl.ds(192, 64)], shifted(-1, -1)),
    ]
    xr[0, pl.ds(0, 192), :] = xs[1, pl.ds(64, 192), :]

    get_qkv4.wait()
    for j in range(3):
        wa[:, pl.ds(128 * j, 128)] = jnp.concatenate(
            [wtmp[j].astype(F32), jnp.zeros((1536, 32), F32)], 1
        ).astype(BF)
    get_proj4.wait()
    for s in range(4):
        wp[s, pl.ds(96, 32), :] = jnp.zeros((32, 1536), BF)

    def column(s):
        return pl.ds(384 * s, 384)

    def both_ways(own, away, cut):
        up, down = pl.ds(0, cut), pl.ds(cut, cut)
        return (
            w.go(own(0, up), away(2, up), along_y(1)),
            w.go(own(0, down), away(2, down), along_y(-1)),
            w.go(own(0, pl.ds(0, 2 * cut)), away(1, pl.ds(0, 2 * cut)), other_core()),
        )

    def pass_on(piece, cut, flight):
        up, down = pl.ds(0, cut), pl.ds(cut, cut)
        flight[0].wait_recv()
        a = w.go(piece(2, up), piece(3, up), other_core())
        flight[1].wait_recv()
        b = w.go(piece(2, down), piece(3, down), other_core())
        return a, b

    def piece_a(s, rows):
        return wa.at[rows, column(s)]

    def piece_p(s, rows):
        return wp.at[s, rows]

    def piece_u(s, rows):
        return wu.at[rows, column(s)]

    def piece_d(s, rows):
        return wd.at[pl.ds(384 * s + rows.start, rows.size)]

    flight_a = both_ways(piece_a, piece_a, 768)
    flight_p = both_ways(piece_p, piece_p, 48)

    moved = table_rows(small_ref[pl.ds(24, 3)].reshape(96, 128))
    lane = iota((1, 256), 1)
    for h in range(3):
        row = head_row(moved, h)
        for m in range(4):
            tabs[0, h, pl.ds(m, 1), :] = row[:, 256 * m : 256 * m + 256]
    tabs[0, 0, pl.ds(4, 1), :] = jnp.where(
        lane < HD, scale4_ref[0], jnp.where(lane < 2 * HD, scale4_ref[1], scale4_ref[2])
    )
    flight_t = [
        w.go(tabs.at[0], tabs.at[1], quad(1, 0)),
        w.go(tabs.at[0], tabs.at[2], quad(0, 1)),
        w.go(tabs.at[0], tabs.at[3], quad(1, 1)),
    ]

    token = iota((512, 32), 0)
    rows = jnp.where(lax.rem(token, 256) // 8 == iota((512, 32), 1), 1.0, 0.0).astype(BF)
    labels = dot(rows, small_ref[27].astype(BF))
    token = iota((512, 128), 0)
    at = iota((512, 128), 1)
    labels = jnp.where(at == token // 256 * 8 + lax.rem(token, 8), labels, 0.0).astype(BF)
    labels = dot(labels, jnp.ones((128, 128), BF))
    aug[...] = jnp.where((labels == at.astype(F32)) | (at == 64), 1.0, 0.0).astype(BF)

    def build3(g, carry):
        moved = table_rows(small_ref[pl.ds(4 * g, 4)].reshape(128, 128))
        for h in range(4):
            row = head_row(moved, h)
            tables = bias_tables([row[:, 256 * m : 256 * m + 256] for m in range(4)])
            for t in range(3):
                for a in range(16):
                    bias3[4 * g + h, t, pl.ds(8 * a, 8), :] = bias_block(tables[t], a)
        return carry

    lax.fori_loop(0, 6, build3, 0)

    get_qkv3.wait()
    for c in halo:
        c.wait_recv()
    x = xr[...].reshape(512, 768)
    square = head_blocks()
    lane = iota((1, 256), 1) // HD
    for j in range(3):
        out = dot(x, wqkv[:, pl.ds(768 * j, 768)]).astype(BF)
        for n in range(3):
            value = out[:, 256 * n : 256 * n + 256]
            if j < 2:
                value = value.astype(F32)
                factor = inverse_norms(value, square)
                if j == 0:
                    row = jnp.zeros((1, 256), F32)
                    for h in range(8):
                        row = jnp.where(lane == h, scale3_ref[8 * n + h], row)
                    factor = factor * row
                value = (value * factor).astype(BF)
            qkv[6 * j + 2 * n] = value[:, :128]
            qkv[6 * j + 2 * n + 1] = value[:, 128:]

    masks = head_masks(4)
    lane = iota((1, 128), 1)
    level = jnp.where(lane < 64, MASK, -MASK).astype(BF)

    def group(g, carry):
        for win in range(2):

            def rows(ref_at):
                return jnp.concatenate(
                    [ref_at(pl.ds(128 * win, 128)), ref_at(pl.ds(256 + 128 * win, 128))], 0
                )

            q, k, v = (rows(lambda r, j=j: qkv[6 * j + g, r, :]) for j in range(3))
            marks = rows(lambda r: aug[r, :])
            keys = jnp.concatenate([k, marks], 1)
            marks = marks * level
            right = jnp.concatenate([v, jnp.ones((256, 128), BF)], 1)
            outs = []
            for h in range(4):
                score = dot_nt(jnp.concatenate([q * masks[h], marks], 1), keys)
                level_h = bias3[4 * g + h, 1]
                spot = jnp.concatenate(
                    [
                        jnp.concatenate([level_h, bias3[4 * g + h, 2]], 1),
                        jnp.concatenate([bias3[4 * g + h, 0], level_h], 1),
                    ],
                    0,
                )
                outs.append(dot(jnp.exp(score + spot).astype(BF), right))
            out = lane_pick([o[:, :128] for o in outs]) / lane_pick([o[:, 128:] for o in outs])
            out = out.astype(BF)
            cols = pl.ds(pl.multiple_of(g * 128, 128), 128)
            ctx[pl.ds(128 * win, 128), cols] = out[:128]
            ctx[pl.ds(256 + 128 * win, 128), cols] = out[128:]
        return carry

    lax.fori_loop(0, 6, group, 0, unroll=2)

    get_up.wait()
    get_down.wait()
    flight_u = both_ways(piece_u, piece_u, 768)
    flight_d = both_ways(piece_d, piece_d, 192)
    late = list(pass_on(piece_a, 768, flight_a) + pass_on(piece_p, 48, flight_p))

    get_proj3.wait()
    y = dot(ctx[...], wproj[...])
    y = layer_norm(y, gain_attn3[...].reshape(1, 768)) + x.astype(F32)
    y = y.astype(BF).astype(F32)
    for half in range(2):
        for r in range(32):
            source = half * 256 + 8 * r
            for m in range(6):
                flat[m, pl.ds(r * 16 + half * 8, 8), :] = y[
                    source : source + 8, 128 * m : 128 * m + 128
                ]
    pieces = []
    for j in range(2):
        side = jnp.concatenate(
            [flat[m, pl.ds(j, 256, stride=2), :] for m in range(6)], 1
        ).reshape(16, 2, 8, 768)
        for i in range(2):
            pieces.append(side[:, i].reshape(128, 768).astype(BF))
    get_merge.wait()
    merged = dot(jnp.concatenate(pieces, 1), wm[...])
    merged = layer_norm(merged, gain_merge[...].reshape(1, 1536)).astype(BF)
    row, col = iota((128, 128), 0), iota((128, 128), 1)
    source = lax.rem(row, 64) // 4 * 8 + row // 64 * 4 + lax.rem(row, 4)
    order = jnp.where(col == source, 1.0, 0.0).astype(BF)
    m4[...] = dot(order, merged).astype(BF).reshape(2, 64, 1536)

    shift = [
        w.go(m4.at[1, pl.ds(0, 48)], back.at[pl.ds(16, 48)], shifted(0, 1)),
        w.go(m4.at[0, pl.ds(48, 16)], back.at[pl.ds(64, 16)], shifted(1, 0)),
        w.go(m4.at[1, pl.ds(48, 16)], back.at[pl.ds(0, 16)], shifted(1, 1)),
    ]
    back[pl.ds(80, 48), :] = m4[0, pl.ds(0, 48), :]
    for c in flight_t:
        c.wait_recv()

    def build4(n, carry):
        s, h = n // 3, lax.rem(n, 3)
        rows = tabs[s, h]
        tables = bias_tables([rows[m : m + 1] for m in range(4)])
        side = jnp.where(core == 0, tables[2], tables[0])
        for a in range(16):
            bias4[n, pl.ds(8 * a, 8), pl.ds(0, 128)] = bias_block(tables[1], a)
            bias4[n, pl.ds(8 * a, 8), pl.ds(128, 128)] = bias_block(side, a)
        return carry

    lax.fori_loop(0, 12, build4, 0)
    for c in shift:
        c.wait_recv()
    source = lax.rem(row, 8) // 4 * 64 + row // 8 * 4 + lax.rem(row, 4)
    order = jnp.where(col == source, 1.0, 0.0).astype(BF)
    blocks[0] = dot(order, back[...]).astype(BF)

    def attend(b):
        both = jnp.concatenate([blocks[b], others[b]], 0)
        qkv4[...] = dot(both, wa[...]).astype(BF)
        outs = []
        for pair in range(2):
            normed = []
            for n in range(3):
                value = qkv4[:, pl.ds(768 * pair + 256 * n, 256)]
                full = value.astype(F32)
                full = full * inverse_norms(full, square)
                for i in range(2):
                    part_of = slice(128 * i, 128 * i + 128)
                    kind = (2 * n + i) % 3
                    normed.append(value[:, part_of] if kind == 2 else full[:, part_of])
            for s in range(2):
                q, k, v = normed[3 * s : 3 * s + 3]
                q = (q[:128] * tabs[2 * pair + s, 0, pl.ds(4, 1), pl.ds(0, 128)]).astype(BF)
                k = k.astype(BF)
                right = jnp.concatenate([v, jnp.ones((256, 128), BF)], 1)
                sums = []
                for h in range(3):
                    score = dot_nt(q * masks[h], k) + bias4[3 * (2 * pair + s) + h]
                    sums.append(dot(jnp.exp(score).astype(BF), right))
                outs.append(
                    (
                        lane_pick([o[:, :128] for o in sums])
                        / lane_pick([o[:, 128:] for o in sums])
                    ).astype(BF)
                )
        part[b] = dot(jnp.concatenate(outs, 1), wp[...].reshape(512, 1536)).astype(BF)

    def feed(b):
        inner = gelu(dot(hidden[b], wu[...])).astype(BF)
        part[b] = dot(inner, wd[...]).astype(BF)

    def ring(held, buf, compute, meet, between):
        right = w.go(held.at[0], held.at[1], along_x(1))
        left = w.go(held.at[0], held.at[2], along_x(-1))
        meet(0)
        compute(0)
        right.wait_recv()
        on_right = w.go(held.at[1, first], held.at[3, first], along_x(1))
        left.wait_recv()
        on_left = w.go(held.at[2, second], held.at[3, second], along_x(-1))
        meet(1)
        compute(1)
        near_left = w.go(part.at[1], buf.at[0], along_x(-1))
        meet(2)
        compute(2)
        near_right = w.go(part.at[2], buf.at[1], along_x(1))
        on_right.wait_recv()
        on_left.wait_recv()
        meet(3)
        compute(3)
        far = w.go(part.at[3], buf.at[2], along_x(2))
        between()
        total = part[0].astype(F32)
        near_left.wait_recv()
        near_right.wait_recv()
        total = total + buf[0].astype(F32) + buf[1].astype(F32)
        far.wait_recv()
        total = total + buf[2].astype(F32)
        for c in (right, left, on_right, on_left, near_left, near_right, far):
            c.wait_send()
        return total

    crossing = []

    def meet_core(b):
        if b == 0:
            crossing.append(w.go(blocks.at[0], others.at[0], other_core()))
            for flight in (flight_a, flight_p):
                flight[2].wait_recv()
            for c in late:
                c.wait_recv()
        if b == 1:
            crossing.append(w.go(blocks.at[1], others.at[1], other_core()))
            crossing.append(w.go(blocks.at[2], others.at[2], other_core()))
        if b == 3:
            crossing.append(w.go(blocks.at[3], others.at[3], other_core()))
        crossing[b].wait_recv()

    later = []

    def pass_mlp():
        later.extend(pass_on(piece_u, 768, flight_u) + pass_on(piece_d, 192, flight_d))

    total = ring(blocks, buf4, attend, meet_core, pass_mlp)
    total = layer_norm(total, gain_attn4[...].reshape(1, 1536))
    hidden[0] = (blocks[0].astype(F32) + total).astype(BF)

    def meet_weights(b):
        if b == 0:
            for flight in (flight_u, flight_d):
                flight[2].wait_recv()
            for c in later:
                c.wait_recv()

    def settle():
        for c in halo + shift + flight_t + crossing + late + later:
            c.wait_send()
        for flight in (flight_a, flight_p, flight_u, flight_d):
            for c in flight:
                c.wait_send()

    total = ring(hidden, bufm, feed, meet_weights, settle)
    total = layer_norm(total, gain_mlp4[...].reshape(1, 1536))
    out_ref[...] = (hidden[0].astype(F32) + total).astype(BF).reshape(16, 8, 1536)


def per_device(
    tokens,
    regions,
    w_qkv3,
    w_proj3,
    bias_table3,
    logit_scale3,
    gain_attn3,
    w_merge,
    gain_merge,
    w_qkv4,
    w_proj4,
    bias_table4,
    logit_scale4,
    gain_attn4,
    w_up4,
    w_down4,
    gain_mlp4,
):
    small = jnp.concatenate(
        [
            jnp.pad(bias_table3, ((0, 0), (0, 1), (0, 97))),
            jnp.pad(bias_table4, ((0, 0), (0, 1), (0, 97))),
            jnp.pad(regions.astype(F32)[None], ((0, 0), (0, 0), (0, 112))),
        ],
        0,
    )
    any_ = pl.BlockSpec(memory_space=pl.ANY)
    vm = pl.BlockSpec(memory_space=pltpu.VMEM)
    sm = pl.BlockSpec(memory_space=pltpu.SMEM)
    out = pl.pallas_call(
        whole_kernel,
        name="whole",
        out_shape=jax.ShapeDtypeStruct((16, 8, 1536), BF),
        in_specs=[any_, vm, sm, sm, any_, any_, vm, any_, vm, any_, any_, vm, any_, any_, vm],
        out_specs=vm,
        scratch_shapes=[
            pltpu.VMEM((512, 768), BF),
            pltpu.VMEM((2, 256, 768), BF),
            pltpu.VMEM((2, 256, 768), BF),
            pltpu.VMEM((512, 128), BF),
            pltpu.VMEM((768, 2304), BF),
            pltpu.VMEM((768, 768), BF),
            pltpu.VMEM((3072, 1536), BF),
            pltpu.VMEM((18, 512, 128), BF),
            pltpu.VMEM((24, 3, 128, 128), F32),
            pltpu.VMEM((6, 512, 128), F32),
            pltpu.VMEM((2, 64, 1536), BF),
            pltpu.VMEM((128, 1536), BF),
            pltpu.VMEM((4, 3, 8, 256), F32),
            pltpu.VMEM((12, 128, 256), F32),
            pltpu.VMEM((3, 1536, 96), BF),
            pltpu.VMEM((1536, 1536), BF),
            pltpu.VMEM((4, 128, 1536), BF),
            pltpu.VMEM((4, 128, 1536), BF),
            pltpu.VMEM((4, 128, 1536), BF),
            pltpu.VMEM((256, 1536), BF),
            pltpu.VMEM((4, 128, 1536), BF),
            pltpu.VMEM((3, 128, 1536), BF),
            pltpu.VMEM((3, 128, 1536), BF),
            pltpu.VMEM((4, 128, 1536), BF),
            pltpu.VMEM((1536, 1536), BF),
            pltpu.VMEM((1536, 1536), BF),
            pltpu.SemaphoreType.DMA((WIRES,)),
            pltpu.SemaphoreType.DMA((WIRES,)),
            pltpu.SemaphoreType.DMA((8,)),
        ],
        compiler_params=pltpu.CompilerParams(
            collective_id=1, has_side_effects=True, vmem_limit_bytes=VMEM_LIMIT
        ),
    )(
        tokens.reshape(512, 768),
        small,
        logit_scale3,
        logit_scale4,
        w_qkv3,
        w_proj3,
        gain_attn3,
        w_merge,
        gain_merge,
        w_qkv4,
        w_proj4,
        gain_attn4,
        w_up4,
        w_down4,
        gain_mlp4,
    )
    return out

def solution(mesh):
    placed = (
        P("wide", "narrow", None),
        P("wide", "narrow"),
        P(),
        P(),
        P(),
        P(),
        P(),
        P(),
        P(),
        P(None, None, "narrow"),
        P("narrow", None),
        P("narrow", None, None),
        P("narrow"),
        P(),
        P(None, "narrow"),
        P("narrow", None),
        P(),
    )
    return jax.shard_map(
        per_device, mesh=mesh, in_specs=placed, out_specs=P("wide", "narrow", None), check_vma=False
    )
```

```python
import jax
import jax.numpy as jnp
from jax import lax
from jax.experimental import pallas as pl
from jax.experimental.pallas import tpu as pltpu
from jax.sharding import PartitionSpec as P

HD = 32
MESH = pl.DeviceIdType.MESH
BF = jnp.bfloat16
F32 = jnp.float32
MASK = 100.0
WIRES = 128
VMEM_LIMIT = 61 << 20


def place():
    wide, narrow = lax.axis_index("wide"), lax.axis_index("narrow")
    return wide, narrow


def shifted(dw, dn):
    wide, narrow = place()
    return (lax.rem(wide + dw + 8, 8), lax.rem(narrow + dn + 16, 16))


def along_x(step):
    wide, narrow = place()
    return (wide, lax.rem(narrow + 4 * step + 16, 16))


def along_y(step):
    wide, narrow = place()
    y = (wide // 4) * 2 + lax.rem(narrow // 2, 2)
    y = lax.rem(y + step + 4, 4)
    return (
        (y // 2) * 4 + lax.rem(wide, 4),
        (narrow // 4) * 4 + lax.rem(y, 2) * 2 + lax.rem(narrow, 2),
    )


def along_z(step):
    wide, narrow = place()
    return ((wide // 4) * 4 + lax.rem(wide + step + 4, 4), narrow)


def other_core():
    wide, narrow = place()
    return (wide, narrow + 1 - 2 * lax.rem(narrow, 2))


def quad(core, row):
    wide, narrow = place()
    c, r = lax.rem(narrow, 2), lax.rem(narrow // 2, 2)
    c = 1 - c if core else c
    r = 1 - r if row else r
    return (wide, (narrow // 4) * 4 + r * 2 + c)


def greet(sources, expected):
    barrier = pltpu.get_barrier_semaphore()
    for device in sources:
        pl.semaphore_signal(barrier, inc=1, device_id=device, device_id_type=MESH)
    pl.semaphore_wait(barrier, expected)


class Wires:
    def __init__(self, send, recv):
        self.send, self.recv, self.count = send, recv, 0

    def copy(self, src, dst, device):
        i = self.count
        self.count += 1
        out = pltpu.make_async_remote_copy(
            src_ref=src,
            dst_ref=dst,
            send_sem=self.send.at[i],
            recv_sem=self.recv.at[i],
            device_id=device,
            device_id_type=MESH,
        )
        return out

    def go(self, src, dst, device):
        out = self.copy(src, dst, device)
        out.start()
        return out


def dot(a, b):
    return jnp.dot(a, b, preferred_element_type=F32)


def dot_nt(a, b):
    return lax.dot_general(a, b, (((1,), (1,)), ((), ())), preferred_element_type=F32)


def iota(shape, axis):
    return lax.broadcasted_iota(jnp.int32, shape, axis)


def layer_norm(values, gain):
    center = jnp.mean(values, -1, keepdims=True)
    offset = values - center
    spread = jnp.mean(offset * offset, -1, keepdims=True)
    return offset * lax.rsqrt(spread + 1e-05) * gain


def gelu(x):
    return 0.5 * x * (1.0 + lax.erf(x * (2.0**-0.5)))


def head_blocks():
    same = iota((256, 256), 0) // HD == iota((256, 256), 1) // HD
    return jnp.where(same, 1.0, 0.0).astype(BF)


def inverse_norms(values, blocks):
    return lax.rsqrt(dot((values * values).astype(BF), blocks) + 1e-06)


def lane_pick(values):
    lane = iota((1, 128), 1)
    out = values[0]
    for h in range(1, len(values)):
        out = jnp.where(lane >= h * HD, values[h], out)
    return out


def head_masks(count):
    lane = iota((1, 128), 1) // HD
    return [jnp.where(lane == h, 1.0, 0.0).astype(BF) for h in range(count)]


def table_rows(tables):
    lane = iota((256, 1024), 1)
    spot = lax.rem(iota((256, 1024), 0), 128)
    pick = jnp.where(spot == 31 - 8 * (lane // 256) - lax.rem(lane, 8), 1.0, 0.0).astype(BF)
    high = tables.astype(BF)
    low = (tables - high.astype(F32)).astype(BF)
    moved = dot(jnp.concatenate([high, low], 1), pick)
    row = lax.rem(iota(moved.shape, 0), 32)
    f = lax.rem(iota(moved.shape, 1), 256) // 8
    return jnp.where(row == 30 - f, moved, 0.0)


def head_row(moved, head):
    values = jnp.sum(moved[32 * head : 32 * head + 32], 0, keepdims=True)
    return 16.0 / (1.0 + jnp.exp(-values))


def bias_tables(rows):
    sub = iota((8, 256), 0)
    lane = lax.rem(iota((8, 256), 1), 8)
    spread = [jnp.broadcast_to(r, (8, 256)) for r in rows]
    tables = []
    for m in range(1, 4):
        straight = pltpu.roll(spread[m], 0, 1, stride=1, stride_axis=0)
        around = pltpu.roll(spread[m - 1], 248, 1, stride=1, stride_axis=0)
        tables.append(jnp.where(lane >= sub, straight, around))
    return tables


def bias_block(table, a):
    return pltpu.roll(table, (256 - 8 * (15 - a)) % 256, 1)[:, :128]


def whole_kernel(
    tokens_ref,
    small_ref,
    scale3_ref,
    scale4_ref,
    wqkv3_hbm,
    wproj3_hbm,
    gain_attn3,
    wm_hbm,
    gain_merge,
    wqkv4_hbm,
    wproj4_hbm,
    gain_attn4,
    wup_hbm,
    wdown_hbm,
    gain_mlp4,
    out_ref,
    ctx,
    xs,
    xr,
    aug,
    wqkv,
    wproj,
    wm,
    qkv,
    bias3,
    tabs,
    wtmp,
    wa,
    wp,
    blocks,
    others,
    buf4,
    visit,
    wu,
    wd,
    send,
    recv,
    local,
):
    w = Wires(send, recv)
    core = lax.rem(lax.axis_index("narrow"), 2)
    first, second = pl.ds(0, 64), pl.ds(64, 64)
    part = [wqkv.at[pl.ds(128 * b, 128), pl.ds(0, 1536)] for b in range(4)]
    qkv4 = wqkv.at[pl.ds(512, 256), pl.ds(0, 1536)]
    visit_part = part[0]
    back, hidden, bufm = visit, others.at[0], buf4.at[0]

    def bias_rows(n, t, start=0, size=128):
        return pl.ds(pl.multiple_of((3 * n + t) * 128 + start, 8), size)

    loads = []
    for i, (src, dst) in enumerate(
        (
            (tokens_ref, ctx),
            (wqkv4_hbm, wtmp),
            (wproj4_hbm, wp.at[0, pl.ds(0, 96)]),
            (wqkv3_hbm, wqkv),
            (wproj3_hbm, wproj),
            (wm_hbm, wm),
            (wup_hbm, wu.at[:, pl.ds(0, 384)]),
            (wdown_hbm, wd.at[pl.ds(0, 384)]),
        )
    ):
        load = pltpu.make_async_copy(src, dst, local.at[i])
        load.start()
        loads.append(load)
    get_tokens, get_qkv4, get_proj4, get_qkv3, get_proj3, get_merge, get_up, get_down = loads

    partners = [shifted(i, j) for i, j in ((0, 1), (1, 0), (1, 1), (0, -1), (-1, 0), (-1, -1))]
    partners += [quad(1, 0), quad(0, 1), quad(1, 1), along_x(1), along_x(-1), along_x(2)]
    partners += [along_y(1), along_y(-1), along_z(1), along_z(-1)]
    greet(partners, len(partners))

    get_tokens.wait()
    grouped = ctx[...].astype(F32).reshape(32, 2, 8, 768)
    for half in range(2):
        xs[half] = grouped[:, half].reshape(256, 768).astype(BF)
    halo = [
        w.go(xs.at[0, pl.ds(64, 192)], xr.at[1, pl.ds(0, 192)], shifted(0, -1)),
        w.go(xs.at[1, pl.ds(0, 64)], xr.at[0, pl.ds(192, 64)], shifted(-1, 0)),
        w.go(xs.at[0, pl.ds(0, 64)], xr.at[1, pl.ds(192, 64)], shifted(-1, -1)),
    ]
    xr[0, pl.ds(0, 192), :] = xs[1, pl.ds(64, 192), :]

    get_qkv4.wait()
    for j in range(3):
        wa[:, pl.ds(128 * j, 128)] = jnp.concatenate(
            [wtmp[j].astype(F32), jnp.zeros((1536, 32), F32)], 1
        ).astype(BF)
    get_proj4.wait()
    for s in range(4):
        wp[s, pl.ds(96, 32), :] = jnp.zeros((32, 1536), BF)

    def column(s):
        return pl.ds(384 * s, 384)

    def both_ways(own, away, cut):
        up, down = pl.ds(0, cut), pl.ds(cut, cut)
        return (
            w.go(own(0, up), away(2, up), along_y(1)),
            w.go(own(0, down), away(2, down), along_y(-1)),
            w.go(own(0, pl.ds(0, 2 * cut)), away(1, pl.ds(0, 2 * cut)), other_core()),
        )

    def pass_on(piece, cut, flight):
        up, down = pl.ds(0, cut), pl.ds(cut, cut)
        flight[0].wait_recv()
        a = w.go(piece(2, up), piece(3, up), other_core())
        flight[1].wait_recv()
        b = w.go(piece(2, down), piece(3, down), other_core())
        return a, b

    def piece_a(s, rows):
        return wa.at[rows, column(s)]

    def piece_p(s, rows):
        return wp.at[s, rows]

    plane = lax.rem(lax.axis_index("wide"), 4)

    def eighths(slot, start, count):
        down = pl.multiple_of(48 * start, 48)
        if slot is None:
            return (
                wup_hbm.at[pl.ds(pl.multiple_of(192 * start, 192), 192 * count)],
                wdown_hbm.at[pl.ds(down, 48 * count)],
            )
        return (
            wu.at[pl.ds(pl.multiple_of(192 * start, 192), 192 * count), column(slot)],
            wd.at[pl.ds(384 * slot + down, 48 * count)],
        )

    def send_mlp(source, target, start, count, device):
        return [
            w.go(a, b, device)
            for a, b in zip(eighths(source, start, count), eighths(target, start, count))
        ]

    def arrive(copies):
        for c in copies:
            c.wait_recv()

    def quarter(step):
        return 2 * lax.rem(plane + step + 4, 4)

    def spread_z(slot):
        return (
            send_mlp(slot, slot, quarter(0), 2, along_z(1)),
            send_mlp(slot, slot, quarter(0), 2, along_z(-1)),
        )

    def forward_z(slot, flight):
        arrive(flight[0])
        a = send_mlp(slot, slot, quarter(-1), 1, along_z(1))
        arrive(flight[1])
        b = send_mlp(slot, slot, quarter(1) + 1, 1, along_z(-1))
        c = send_mlp(slot, slot + 1, quarter(-1), 2, other_core())
        c += send_mlp(slot, slot + 1, quarter(1), 2, other_core())
        return a + b, c

    moved = table_rows(small_ref[pl.ds(24, 3)].reshape(96, 128))
    lane = iota((1, 256), 1)
    for h in range(3):
        row = head_row(moved, h)
        for m in range(4):
            tabs[0, h, pl.ds(m, 1), :] = row[:, 256 * m : 256 * m + 256]
    tabs[0, 0, pl.ds(4, 1), :] = jnp.where(
        lane < HD, scale4_ref[0], jnp.where(lane < 2 * HD, scale4_ref[1], scale4_ref[2])
    )
    flight_t = [
        w.go(tabs.at[0], tabs.at[1], quad(1, 0)),
        w.go(tabs.at[0], tabs.at[2], quad(0, 1)),
        w.go(tabs.at[0], tabs.at[3], quad(1, 1)),
    ]

    token = iota((512, 32), 0)
    rows = jnp.where(lax.rem(token, 256) // 8 == iota((512, 32), 1), 1.0, 0.0).astype(BF)
    labels = dot(rows, small_ref[27].astype(BF))
    token = iota((512, 128), 0)
    at = iota((512, 128), 1)
    labels = jnp.where(at == token // 256 * 8 + lax.rem(token, 8), labels, 0.0).astype(BF)
    labels = dot(labels, jnp.ones((128, 128), BF))
    aug[...] = jnp.where((labels == at.astype(F32)) | (at == 64), 1.0, 0.0).astype(BF)

    def build3(g, carry):
        moved = table_rows(small_ref[pl.ds(4 * g, 4)].reshape(128, 128))
        for h in range(4):
            row = head_row(moved, h)
            tables = bias_tables([row[:, 256 * m : 256 * m + 256] for m in range(4)])
            for t in range(3):
                for a in range(16):
                    bias3[bias_rows(4 * g + h, t, 8 * a, 8), :] = bias_block(tables[t], a)
        return carry

    lax.fori_loop(0, 6, build3, 0)

    get_qkv3.wait()
    for c in halo:
        c.wait_recv()
    flight_a = both_ways(piece_a, piece_a, 768)
    flight_p = both_ways(piece_p, piece_p, 48)
    across = send_mlp(None, 4, quarter(0), 2, along_x(2))
    x = xr[...].reshape(512, 768)
    square = head_blocks()
    lane = iota((1, 256), 1) // HD
    for j in range(3):
        out = dot(x, wqkv[:, pl.ds(768 * j, 768)]).astype(BF)
        for n in range(3):
            value = out[:, 256 * n : 256 * n + 256]
            if j < 2:
                value = value.astype(F32)
                factor = inverse_norms(value, square)
                if j == 0:
                    row = jnp.zeros((1, 256), F32)
                    for h in range(8):
                        row = jnp.where(lane == h, scale3_ref[8 * n + h], row)
                    factor = factor * row
                value = (value * factor).astype(BF)
            qkv[6 * j + 2 * n] = value[:, :128]
            qkv[6 * j + 2 * n + 1] = value[:, 128:]

    masks = head_masks(4)
    lane = iota((1, 128), 1)
    level = jnp.where(lane < 64, MASK, -MASK).astype(BF)

    def group(g, carry):
        for win in range(2):

            def rows(ref_at):
                return jnp.concatenate(
                    [ref_at(pl.ds(128 * win, 128)), ref_at(pl.ds(256 + 128 * win, 128))], 0
                )

            q, k, v = (rows(lambda r, j=j: qkv[6 * j + g, r, :]) for j in range(3))
            marks = rows(lambda r: aug[r, :])
            keys = jnp.concatenate([k, marks], 1)
            marks = marks * level
            right = jnp.concatenate([v, jnp.ones((256, 128), BF)], 1)
            outs = []
            for h in range(4):
                score = dot_nt(jnp.concatenate([q * masks[h], marks], 1), keys)
                side = [bias3[bias_rows(4 * g + h, t), :] for t in range(3)]
                spot = jnp.concatenate(
                    [
                        jnp.concatenate([side[1], side[2]], 1),
                        jnp.concatenate([side[0], side[1]], 1),
                    ],
                    0,
                )
                outs.append(dot(jnp.exp(score + spot).astype(BF), right))
            out = lane_pick([o[:, :128] for o in outs]) / lane_pick([o[:, 128:] for o in outs])
            out = out.astype(BF)
            cols = pl.ds(pl.multiple_of(g * 128, 128), 128)
            ctx[pl.ds(128 * win, 128), cols] = out[:128]
            ctx[pl.ds(256 + 128 * win, 128), cols] = out[128:]
        return carry

    lax.fori_loop(0, 6, group, 0, unroll=2)

    get_proj3.wait()
    y = dot(ctx[...], wproj[...])
    y = layer_norm(y, gain_attn3[...].reshape(1, 768)) + x.astype(F32)
    y = y.astype(BF).astype(F32)
    for half in range(2):
        for r in range(32):
            source = half * 256 + 8 * r
            for m in range(6):
                bias3[pl.ds(512 * m + r * 16 + half * 8, 8), :] = y[
                    source : source + 8, 128 * m : 128 * m + 128
                ]
    pieces = []
    for j in range(2):
        side = jnp.concatenate(
            [bias3[pl.ds(512 * m + j, 256, stride=2), :] for m in range(6)], 1
        ).reshape(16, 2, 8, 768)
        for i in range(2):
            pieces.append(side[:, i].reshape(128, 768).astype(BF))
    get_merge.wait()
    merged = dot(jnp.concatenate(pieces, 1), wm[...])
    merged = layer_norm(merged, gain_merge[...].reshape(1, 1536)).astype(BF)
    row, col = iota((128, 128), 0), iota((128, 128), 1)
    source = lax.rem(row, 64) // 4 * 8 + row // 64 * 4 + lax.rem(row, 4)
    order = jnp.where(col == source, 1.0, 0.0).astype(BF)
    m4 = part[0]
    m4[...] = dot(order, merged).astype(BF)

    shift = [
        w.go(m4.at[pl.ds(64, 48)], back.at[pl.ds(16, 48)], shifted(0, 1)),
        w.go(m4.at[pl.ds(48, 16)], back.at[pl.ds(64, 16)], shifted(1, 0)),
        w.go(m4.at[pl.ds(112, 16)], back.at[pl.ds(0, 16)], shifted(1, 1)),
    ]
    back[pl.ds(80, 48), :] = m4[pl.ds(0, 48), :]
    for c in flight_t:
        c.wait_recv()

    def build4(n, carry):
        s, h = n // 3, lax.rem(n, 3)
        rows = tabs[s, h]
        tables = bias_tables([rows[m : m + 1] for m in range(4)])
        side = jnp.where(core == 0, tables[2], tables[0])
        for a in range(16):
            bias3[bias_rows(n, 0, 8 * a, 8), :] = bias_block(tables[1], a)
            bias3[bias_rows(n, 1, 8 * a, 8), :] = bias_block(side, a)
        return carry

    lax.fori_loop(0, 12, build4, 0)
    for c in shift:
        c.wait()
    late = list(pass_on(piece_a, 768, flight_a) + pass_on(piece_p, 48, flight_p))
    arrive(across)
    spread4 = spread_z(4)
    skew = send_mlp(4, 6, quarter(0), 1, along_y(1))
    skew += send_mlp(4, 6, quarter(0) + 1, 1, along_y(-1))
    mates = send_mlp(4, 5, quarter(0), 2, other_core())
    get_up.wait()
    get_down.wait()
    beside = send_mlp(0, 2, 0, 4, along_y(1))
    beside += send_mlp(0, 2, 4, 4, along_y(-1))
    mates += send_mlp(0, 1, 0, 8, other_core())
    onward = []
    source = lax.rem(row, 8) // 4 * 64 + row // 8 * 4 + lax.rem(row, 4)
    order = jnp.where(col == source, 1.0, 0.0).astype(BF)
    blocks[0] = dot(order, back[...]).astype(BF)

    def attend(b):
        both = jnp.concatenate([blocks[b], others[b]], 0)
        qkv4[...] = dot(both, wa[...]).astype(BF)
        outs = []
        for pair in range(2):
            normed = []
            for n in range(3):
                value = qkv4[:, pl.ds(768 * pair + 256 * n, 256)]
                full = value.astype(F32)
                full = full * inverse_norms(full, square)
                for i in range(2):
                    part_of = slice(128 * i, 128 * i + 128)
                    kind = (2 * n + i) % 3
                    normed.append(value[:, part_of] if kind == 2 else full[:, part_of])
            for s in range(2):
                q, k, v = normed[3 * s : 3 * s + 3]
                q = (q[:128] * tabs[2 * pair + s, 0, pl.ds(4, 1), pl.ds(0, 128)]).astype(BF)
                k = k.astype(BF)
                right = jnp.concatenate([v, jnp.ones((256, 128), BF)], 1)
                sums = []
                for h in range(3):
                    n = 3 * (2 * pair + s) + h
                    spot = jnp.concatenate(
                        [bias3[bias_rows(n, 0), :], bias3[bias_rows(n, 1), :]], 1
                    )
                    score = dot_nt(q * masks[h], k) + spot
                    sums.append(dot(jnp.exp(score).astype(BF), right))
                outs.append(
                    (
                        lane_pick([o[:, :128] for o in sums])
                        / lane_pick([o[:, 128:] for o in sums])
                    ).astype(BF)
                )
        part[b][...] = dot(jnp.concatenate(outs, 1), wp[...].reshape(512, 1536)).astype(BF)

    def ring(held, buf, compute, meet, after):
        right = w.go(held.at[0], held.at[1], along_x(1))
        left = w.go(held.at[0], held.at[2], along_x(-1))
        meet(0)
        compute(0)
        after(0)
        right.wait_recv()
        on_right = w.go(held.at[1, first], held.at[3, first], along_x(1))
        left.wait_recv()
        on_left = w.go(held.at[2, second], held.at[3, second], along_x(-1))
        meet(1)
        compute(1)
        near_left = w.go(part[1], buf.at[0], along_x(-1))
        after(1)
        meet(2)
        compute(2)
        near_right = w.go(part[2], buf.at[1], along_x(1))
        after(2)
        on_right.wait_recv()
        on_left.wait_recv()
        meet(3)
        compute(3)
        far = w.go(part[3], buf.at[2], along_x(2))
        after(3)
        total = part[0][...].astype(F32)
        near_left.wait_recv()
        near_right.wait_recv()
        total = total + buf[0].astype(F32) + buf[1].astype(F32)
        far.wait_recv()
        total = total + buf[2].astype(F32)
        for c in (right, left, on_right, on_left, near_left, near_right, far):
            c.wait_send()
        return total

    crossing = []

    def meet_core(b):
        if b == 0:
            crossing.append(w.go(blocks.at[0], others.at[0], other_core()))
            for flight in (flight_a, flight_p):
                flight[2].wait_recv()
            for c in late:
                c.wait_recv()
        if b == 1:
            crossing.append(w.go(blocks.at[1], others.at[1], other_core()))
            crossing.append(w.go(blocks.at[2], others.at[2], other_core()))
        if b == 3:
            crossing.append(w.go(blocks.at[3], others.at[3], other_core()))
        crossing[b].wait_recv()

    spread6 = []
    ends = []

    def after(b):
        if b == 0:
            arrive(skew)
            spread6.extend(spread_z(6))
            mates.extend(send_mlp(6, 7, quarter(0), 2, other_core()))
        if b == 1:
            a, c = forward_z(4, spread4)
            ends.append((4, a))
            mates.extend(c)
        if b == 3:
            a, c = forward_z(6, spread6)
            ends.append((6, a))
            mates.extend(c)
            arrive(beside)
            mates.extend(send_mlp(2, 3, 0, 8, other_core()))

    total = ring(blocks, buf4, attend, meet_core, after)
    total = layer_norm(total, gain_attn4[...].reshape(1, 1536))
    hidden[...] = (blocks[0].astype(F32) + total).astype(BF)

    visits = [
        w.go(hidden.at[first], visit.at[first], along_x(1)),
        w.go(hidden.at[second], visit.at[second], along_x(-1)),
    ]

    def units(tokens, half):
        return gelu(dot(tokens, wu[:, pl.ds(1536 * half, 1536)])).astype(BF)

    for slot, copies in ends:
        arrive(copies)
        mates.extend(send_mlp(slot, slot + 1, quarter(2), 2, other_core()))
    arrive(mates)
    own = dot(units(hidden[...], 0), wd[pl.ds(0, 1536), :])
    arrive(visits)
    guest = dot(units(visit[...], 0), wd[pl.ds(0, 1536), :])
    inner = units(visit[...], 1)
    returns = []
    for n in range(2):
        cols = pl.ds(768 * n, 768)
        value = guest[:, 768 * n : 768 * n + 768] + dot(inner, wd[pl.ds(1536, 1536), cols])
        visit_part[:, cols] = value.astype(BF)
        returns += [
            w.go(visit_part.at[first, cols], bufm.at[first, cols], along_x(-1)),
            w.go(visit_part.at[second, cols], bufm.at[second, cols], along_x(1)),
        ]
    own = own + dot(units(hidden[...], 1), wd[pl.ds(1536, 1536), :])
    sent = halo + flight_t + crossing + late + across + skew + beside + mates
    for f in spread4 + tuple(spread6) + flight_a + flight_p:
        sent += f if isinstance(f, list) else [f]
    for slot, copies in ends:
        sent += copies
    for c in sent + visits + returns:
        c.wait_send()
    arrive(returns)
    total = layer_norm(own + bufm[...].astype(F32), gain_mlp4[...].reshape(1, 1536))
    out_ref[...] = (hidden[...].astype(F32) + total).astype(BF).reshape(16, 8, 1536)


def per_device(
    tokens,
    regions,
    w_qkv3,
    w_proj3,
    bias_table3,
    logit_scale3,
    gain_attn3,
    w_merge,
    gain_merge,
    w_qkv4,
    w_proj4,
    bias_table4,
    logit_scale4,
    gain_attn4,
    w_up4,
    w_down4,
    gain_mlp4,
):
    small = jnp.concatenate(
        [
            jnp.pad(bias_table3, ((0, 0), (0, 1), (0, 97))),
            jnp.pad(bias_table4, ((0, 0), (0, 1), (0, 97))),
            jnp.pad(regions.astype(F32)[None], ((0, 0), (0, 0), (0, 112))),
        ],
        0,
    )
    any_ = pl.BlockSpec(memory_space=pl.ANY)
    vm = pl.BlockSpec(memory_space=pltpu.VMEM)
    sm = pl.BlockSpec(memory_space=pltpu.SMEM)
    out = pl.pallas_call(
        whole_kernel,
        name="whole",
        out_shape=jax.ShapeDtypeStruct((16, 8, 1536), BF),
        in_specs=[any_, vm, sm, sm, any_, any_, vm, any_, vm, any_, any_, vm, any_, any_, vm],
        out_specs=vm,
        scratch_shapes=[
            pltpu.VMEM((512, 768), BF),
            pltpu.VMEM((2, 256, 768), BF),
            pltpu.VMEM((2, 256, 768), BF),
            pltpu.VMEM((512, 128), BF),
            pltpu.VMEM((768, 2304), BF),
            pltpu.VMEM((768, 768), BF),
            pltpu.VMEM((3072, 1536), BF),
            pltpu.VMEM((18, 512, 128), BF),
            pltpu.VMEM((72 * 128, 128), F32),
            pltpu.VMEM((4, 3, 8, 256), F32),
            pltpu.VMEM((3, 1536, 96), BF),
            pltpu.VMEM((1536, 1536), BF),
            pltpu.VMEM((4, 128, 1536), BF),
            pltpu.VMEM((4, 128, 1536), BF),
            pltpu.VMEM((4, 128, 1536), BF),
            pltpu.VMEM((3, 128, 1536), BF),
            pltpu.VMEM((128, 1536), BF),
            pltpu.VMEM((1536, 3072), BF),
            pltpu.VMEM((3072, 1536), BF),
            pltpu.SemaphoreType.DMA((WIRES,)),
            pltpu.SemaphoreType.DMA((WIRES,)),
            pltpu.SemaphoreType.DMA((8,)),
        ],
        compiler_params=pltpu.CompilerParams(
            collective_id=1, has_side_effects=True, vmem_limit_bytes=VMEM_LIMIT
        ),
    )(
        tokens.reshape(512, 768),
        small,
        logit_scale3,
        logit_scale4,
        w_qkv3,
        w_proj3,
        gain_attn3,
        w_merge,
        gain_merge,
        w_qkv4,
        w_proj4,
        gain_attn4,
        w_up4,
        w_down4,
        gain_mlp4,
    )
    return out

def solution(mesh):
    placed = (
        P("wide", "narrow", None),
        P("wide", "narrow"),
        P(),
        P(),
        P(),
        P(),
        P(),
        P(),
        P(),
        P(None, None, "narrow"),
        P("narrow", None),
        P("narrow", None, None),
        P("narrow"),
        P(),
        P(None, "narrow"),
        P("narrow", None),
        P(),
    )
    return jax.shard_map(
        per_device, mesh=mesh, in_specs=placed, out_specs=P("wide", "narrow", None), check_vma=False
    )
```

```python
import jax
import jax.numpy as jnp
from jax import lax
from jax.experimental import pallas as pl
from jax.experimental.pallas import tpu as pltpu
from jax.sharding import PartitionSpec as P

HD = 32
MESH = pl.DeviceIdType.MESH
BF = jnp.bfloat16
F32 = jnp.float32
MASK = 100.0
WIRES = 128
VMEM_LIMIT = 61 << 20


def place():
    wide, narrow = lax.axis_index("wide"), lax.axis_index("narrow")
    return wide, narrow


def shifted(dw, dn):
    wide, narrow = place()
    return (lax.rem(wide + dw + 8, 8), lax.rem(narrow + dn + 16, 16))


def along_x(step):
    wide, narrow = place()
    return (wide, lax.rem(narrow + 4 * step + 16, 16))


def along_y(step):
    wide, narrow = place()
    y = (wide // 4) * 2 + lax.rem(narrow // 2, 2)
    y = lax.rem(y + step + 4, 4)
    return (
        (y // 2) * 4 + lax.rem(wide, 4),
        (narrow // 4) * 4 + lax.rem(y, 2) * 2 + lax.rem(narrow, 2),
    )


def along_z(step):
    wide, narrow = place()
    return ((wide // 4) * 4 + lax.rem(wide + step + 4, 4), narrow)


def other_core():
    wide, narrow = place()
    return (wide, narrow + 1 - 2 * lax.rem(narrow, 2))


def quad(core, row):
    wide, narrow = place()
    c, r = lax.rem(narrow, 2), lax.rem(narrow // 2, 2)
    c = 1 - c if core else c
    r = 1 - r if row else r
    return (wide, (narrow // 4) * 4 + r * 2 + c)


def greet(sources, expected):
    barrier = pltpu.get_barrier_semaphore()
    for device in sources:
        pl.semaphore_signal(barrier, inc=1, device_id=device, device_id_type=MESH)
    pl.semaphore_wait(barrier, expected)


class Wires:
    def __init__(self, send, recv):
        self.send, self.recv, self.count = send, recv, 0

    def copy(self, src, dst, device):
        i = self.count
        self.count += 1
        out = pltpu.make_async_remote_copy(
            src_ref=src,
            dst_ref=dst,
            send_sem=self.send.at[i],
            recv_sem=self.recv.at[i],
            device_id=device,
            device_id_type=MESH,
        )
        return out

    def go(self, src, dst, device):
        out = self.copy(src, dst, device)
        out.start()
        return out


def dot(a, b):
    return jnp.dot(a, b, preferred_element_type=F32)


def dot_nt(a, b):
    return lax.dot_general(a, b, (((1,), (1,)), ((), ())), preferred_element_type=F32)


def iota(shape, axis):
    return lax.broadcasted_iota(jnp.int32, shape, axis)


def layer_norm(values, gain):
    center = jnp.mean(values, -1, keepdims=True)
    offset = values - center
    spread = jnp.mean(offset * offset, -1, keepdims=True)
    return offset * lax.rsqrt(spread + 1e-05) * gain


def gelu(x):
    return 0.5 * x * (1.0 + lax.erf(x * (2.0**-0.5)))


def head_blocks():
    same = iota((256, 256), 0) // HD == iota((256, 256), 1) // HD
    return jnp.where(same, 1.0, 0.0).astype(BF)


def inverse_norms(values, blocks):
    return lax.rsqrt(dot((values * values).astype(BF), blocks) + 1e-06)


def lane_pick(values):
    lane = iota((1, 128), 1)
    out = values[0]
    for h in range(1, len(values)):
        out = jnp.where(lane >= h * HD, values[h], out)
    return out


def head_masks(count):
    lane = iota((1, 128), 1) // HD
    return [jnp.where(lane == h, 1.0, 0.0).astype(BF) for h in range(count)]


def table_rows(logits, each):
    lane = iota((31, 1024), 1)
    column = 31 - 8 * (lane // 256) - lax.rem(lane, 8)
    pick = jnp.where(iota((31, 1024), 0) == column, 1.0, 0.0).astype(BF)
    high = logits.astype(BF)
    low = (logits - high.astype(F32)).astype(BF)
    moved = dot(high, pick) + dot(low, pick)
    row = iota(moved.shape, 0) // each
    f = lax.rem(iota(moved.shape, 1), 256) // 8
    moved = jnp.where(row == 30 - f, moved, 0.0)
    if each == 1:
        values = jnp.sum(moved, 0, keepdims=True)
    else:
        values = jnp.sum(moved.reshape(31, each, 1024), 0)
    return 16.0 / (1.0 + jnp.exp(-values))


def bias_tables(rows):
    sub = iota((8, 256), 0)
    lane = lax.rem(iota((8, 256), 1), 8)
    spread = [jnp.broadcast_to(r, (8, 256)) for r in rows]
    tables = []
    for m in range(1, 4):
        straight = pltpu.roll(spread[m], 0, 1, stride=1, stride_axis=0)
        around = pltpu.roll(spread[m - 1], 248, 1, stride=1, stride_axis=0)
        tables.append(jnp.where(lane >= sub, straight, around))
    return tables


def bias_block(table, a):
    return pltpu.roll(table, (256 - 8 * (15 - a)) % 256, 1)[:, :128]


def whole_kernel(
    tokens_ref,
    labels_ref,
    table3_ref,
    table4_ref,
    scale3_ref,
    scale4_ref,
    wqkv3_hbm,
    wproj3_hbm,
    gain_attn3,
    wm_hbm,
    gain_merge,
    wqkv4_hbm,
    wproj4_hbm,
    gain_attn4,
    wup_hbm,
    wdown_hbm,
    gain_mlp4,
    out_ref,
    ctx,
    xs,
    xr,
    aug,
    wqkv,
    wproj,
    wm,
    qkv,
    bias3,
    tabs,
    wtmp,
    wa,
    wp,
    blocks,
    others,
    buf4,
    visit,
    wu,
    wd,
    send,
    recv,
    local,
):
    w = Wires(send, recv)
    core = lax.rem(lax.axis_index("narrow"), 2)
    first, second = pl.ds(0, 64), pl.ds(64, 64)
    part = [wqkv.at[pl.ds(128 * b, 128), pl.ds(0, 1536)] for b in range(4)]
    qkv4 = wqkv.at[pl.ds(512, 256), pl.ds(0, 1536)]
    visit_part = part[0]
    back, hidden, bufm = visit, others.at[0], buf4.at[0]

    def bias_rows(n, t, start=0, size=128):
        return pl.ds(pl.multiple_of((3 * n + t) * 128 + start, 8), size)

    loads = []
    for i, (src, dst) in enumerate(
        (
            (tokens_ref, ctx),
            (wqkv4_hbm, wtmp),
            (wproj4_hbm, wp.at[0, pl.ds(0, 96)]),
            (wqkv3_hbm, wqkv),
            (wproj3_hbm, wproj),
            (wm_hbm, wm),
            (wup_hbm, wu.at[:, pl.ds(0, 384)]),
            (wdown_hbm, wd.at[pl.ds(0, 384)]),
        )
    ):
        load = pltpu.make_async_copy(src, dst, local.at[i])
        load.start()
        loads.append(load)
    get_tokens, get_qkv4, get_proj4, get_qkv3, get_proj3, get_merge, get_up, get_down = loads

    partners = [shifted(i, j) for i, j in ((0, 1), (1, 0), (1, 1), (0, -1), (-1, 0), (-1, -1))]
    partners += [quad(1, 0), quad(0, 1), quad(1, 1), along_x(1), along_x(-1), along_x(2)]
    partners += [along_y(1), along_y(-1), along_z(1), along_z(-1)]
    greet(partners, len(partners))

    get_tokens.wait()
    grouped = ctx[...].astype(F32).reshape(32, 2, 8, 768)
    for half in range(2):
        xs[half] = grouped[:, half].reshape(256, 768).astype(BF)
    halo = [
        w.go(xs.at[0, pl.ds(64, 192)], xr.at[1, pl.ds(0, 192)], shifted(0, -1)),
        w.go(xs.at[1, pl.ds(0, 64)], xr.at[0, pl.ds(192, 64)], shifted(-1, 0)),
        w.go(xs.at[0, pl.ds(0, 64)], xr.at[1, pl.ds(192, 64)], shifted(-1, -1)),
    ]
    xr[0, pl.ds(0, 192), :] = xs[1, pl.ds(64, 192), :]

    get_qkv4.wait()
    for j in range(3):
        wide = jnp.concatenate([wtmp[j].astype(F32), jnp.zeros((32, 1536), F32)], 0)
        wa[:, pl.ds(128 * j, 128)] = wide.T.astype(BF)
    get_proj4.wait()
    for s in range(4):
        wp[s, pl.ds(96, 32), :] = jnp.zeros((32, 1536), BF)

    def column(s):
        return pl.ds(384 * s, 384)

    def both_ways(own, away, cut):
        up, down = pl.ds(0, cut), pl.ds(cut, cut)
        return (
            w.go(own(0, up), away(2, up), along_y(1)),
            w.go(own(0, down), away(2, down), along_y(-1)),
            w.go(own(0, pl.ds(0, 2 * cut)), away(1, pl.ds(0, 2 * cut)), other_core()),
        )

    def pass_on(piece, cut, flight):
        up, down = pl.ds(0, cut), pl.ds(cut, cut)
        flight[0].wait_recv()
        a = w.go(piece(2, up), piece(3, up), other_core())
        flight[1].wait_recv()
        b = w.go(piece(2, down), piece(3, down), other_core())
        return a, b

    def piece_a(s, rows):
        return wa.at[rows, column(s)]

    def piece_p(s, rows):
        return wp.at[s, rows]

    plane = lax.rem(lax.axis_index("wide"), 4)

    def eighths(slot, start, count):
        down = pl.multiple_of(48 * start, 48)
        if slot is None:
            return (
                wup_hbm.at[pl.ds(pl.multiple_of(192 * start, 192), 192 * count)],
                wdown_hbm.at[pl.ds(down, 48 * count)],
            )
        return (
            wu.at[pl.ds(pl.multiple_of(192 * start, 192), 192 * count), column(slot)],
            wd.at[pl.ds(384 * slot + down, 48 * count)],
        )

    def send_mlp(source, target, start, count, device):
        return [
            w.go(a, b, device)
            for a, b in zip(eighths(source, start, count), eighths(target, start, count))
        ]

    def arrive(copies):
        for c in copies:
            c.wait_recv()

    def quarter(step):
        return 2 * lax.rem(plane + step + 4, 4)

    def spread_z(slot):
        return (
            send_mlp(slot, slot, quarter(0), 2, along_z(1)),
            send_mlp(slot, slot, quarter(0), 2, along_z(-1)),
        )

    def forward_z(slot, flight):
        arrive(flight[0])
        a = send_mlp(slot, slot, quarter(-1), 1, along_z(1))
        arrive(flight[1])
        b = send_mlp(slot, slot, quarter(1) + 1, 1, along_z(-1))
        c = send_mlp(slot, slot + 1, quarter(-1), 2, other_core())
        c += send_mlp(slot, slot + 1, quarter(1), 2, other_core())
        return a + b, c

    lane = iota((1, 256), 1)
    for h in range(3):
        row = table_rows(table4_ref[h], 1)
        for m in range(4):
            tabs[0, h, pl.ds(m, 1), :] = row[:, 256 * m : 256 * m + 256]
    tabs[0, 0, pl.ds(4, 1), :] = jnp.where(
        lane < HD, scale4_ref[0], jnp.where(lane < 2 * HD, scale4_ref[1], scale4_ref[2])
    )
    flight_t = [
        w.go(tabs.at[0], tabs.at[1], quad(1, 0)),
        w.go(tabs.at[0], tabs.at[2], quad(0, 1)),
        w.go(tabs.at[0], tabs.at[3], quad(1, 1)),
    ]

    token = iota((512, 16), 0)
    pick = token // 256 * 8 + lax.rem(token, 8) == iota((512, 16), 1)
    labels = dot(jnp.where(pick, 1.0, 0.0).astype(BF), labels_ref[...].astype(F32).astype(BF))
    pick = lax.rem(iota((512, 32), 0), 256) // 8 == iota((512, 32), 1)
    labels = jnp.where(pick, labels, 0.0).astype(BF)
    at = iota((512, 128), 1)
    labels = dot(labels, jnp.ones((32, 128), BF))
    aug[...] = jnp.where((labels == at.astype(F32)) | (at == 64), 1.0, 0.0).astype(BF)


    def build3(i, carry):
        heads = pl.ds(pl.multiple_of(8 * i, 8), 8)
        values = table_rows(table3_ref[:, heads, :].reshape(248, 31), 8)
        for h in range(8):
            tables = bias_tables([values[h : h + 1, 256 * m : 256 * m + 256] for m in range(4)])
            for t in range(3):
                for a in range(16):
                    bias3[bias_rows(8 * i + h, t, 8 * a, 8), :] = bias_block(tables[t], a)
        return carry

    lax.fori_loop(0, 3, build3, 0)

    flight_a = both_ways(piece_a, piece_a, 768)
    flight_p = both_ways(piece_p, piece_p, 48)

    get_qkv3.wait()
    for c in halo:
        c.wait_recv()
    across = send_mlp(None, 4, quarter(0), 2, along_x(2))
    x = xr[...].reshape(512, 768)
    square = head_blocks()
    lane = iota((1, 256), 1) // HD
    for j in range(3):
        out = dot(x, wqkv[:, pl.ds(768 * j, 768)]).astype(BF)
        for n in range(3):
            value = out[:, 256 * n : 256 * n + 256]
            if j < 2:
                value = value.astype(F32)
                factor = inverse_norms(value, square)
                if j == 0:
                    row = jnp.zeros((1, 256), F32)
                    for h in range(8):
                        row = jnp.where(lane == h, scale3_ref[8 * n + h], row)
                    factor = factor * row
                value = (value * factor).astype(BF)
            qkv[6 * j + 2 * n] = value[:, :128]
            qkv[6 * j + 2 * n + 1] = value[:, 128:]

    masks = head_masks(4)
    lane = iota((1, 128), 1)
    level = jnp.where(lane < 64, MASK, -MASK).astype(BF)

    def group(g, carry):
        for win in range(2):

            def rows(ref_at):
                return jnp.concatenate(
                    [ref_at(pl.ds(128 * win, 128)), ref_at(pl.ds(256 + 128 * win, 128))], 0
                )

            q, k, v = (rows(lambda r, j=j: qkv[6 * j + g, r, :]) for j in range(3))
            marks = rows(lambda r: aug[r, :])
            keys = jnp.concatenate([k, marks], 1)
            marks = marks * level
            right = jnp.concatenate([v, jnp.ones((256, 128), BF)], 1)
            outs = []
            for h in range(4):
                score = dot_nt(jnp.concatenate([q * masks[h], marks], 1), keys)
                side = [bias3[bias_rows(4 * g + h, t), :] for t in range(3)]
                spot = jnp.concatenate(
                    [
                        jnp.concatenate([side[1], side[2]], 1),
                        jnp.concatenate([side[0], side[1]], 1),
                    ],
                    0,
                )
                outs.append(dot(jnp.exp(score + spot).astype(BF), right))
            out = lane_pick([o[:, :128] for o in outs]) / lane_pick([o[:, 128:] for o in outs])
            out = out.astype(BF)
            cols = pl.ds(pl.multiple_of(g * 128, 128), 128)
            ctx[pl.ds(128 * win, 128), cols] = out[:128]
            ctx[pl.ds(256 + 128 * win, 128), cols] = out[128:]
        return carry

    lax.fori_loop(0, 6, group, 0, unroll=2)

    get_proj3.wait()
    y = dot(ctx[...], wproj[...])
    y = layer_norm(y, gain_attn3[...].reshape(1, 768)) + x.astype(F32)
    y = y.astype(BF).astype(F32)
    for half in range(2):
        for r in range(32):
            source = half * 256 + 8 * r
            for m in range(6):
                bias3[pl.ds(512 * m + r * 16 + half * 8, 8), :] = y[
                    source : source + 8, 128 * m : 128 * m + 128
                ]
    pieces = []
    for j in range(2):
        side = jnp.concatenate(
            [bias3[pl.ds(512 * m + j, 256, stride=2), :] for m in range(6)], 1
        ).reshape(16, 2, 8, 768)
        for i in range(2):
            pieces.append(side[:, i].reshape(128, 768).astype(BF))
    get_merge.wait()
    merged = dot(jnp.concatenate(pieces, 1), wm[...])
    merged = layer_norm(merged, gain_merge[...].reshape(1, 1536)).astype(BF)
    row, col = iota((128, 128), 0), iota((128, 128), 1)
    source = lax.rem(row, 64) // 4 * 8 + row // 64 * 4 + lax.rem(row, 4)
    order = jnp.where(col == source, 1.0, 0.0).astype(BF)
    m4 = part[0]
    m4[...] = dot(order, merged).astype(BF)

    shift = [
        w.go(m4.at[pl.ds(64, 48)], back.at[pl.ds(16, 48)], shifted(0, 1)),
        w.go(m4.at[pl.ds(48, 16)], back.at[pl.ds(64, 16)], shifted(1, 0)),
        w.go(m4.at[pl.ds(112, 16)], back.at[pl.ds(0, 16)], shifted(1, 1)),
    ]
    back[pl.ds(80, 48), :] = m4[pl.ds(0, 48), :]
    for c in flight_t:
        c.wait_recv()

    def build4(n, carry):
        s, h = n // 3, lax.rem(n, 3)
        rows = tabs[s, h]
        tables = bias_tables([rows[m : m + 1] for m in range(4)])
        side = jnp.where(core == 0, tables[2], tables[0])
        for a in range(16):
            bias3[bias_rows(n, 0, 8 * a, 8), :] = bias_block(tables[1], a)
            bias3[bias_rows(n, 1, 8 * a, 8), :] = bias_block(side, a)
        return carry

    lax.fori_loop(0, 12, build4, 0)
    for c in shift:
        c.wait()
    late = list(pass_on(piece_a, 768, flight_a) + pass_on(piece_p, 48, flight_p))
    arrive(across)
    spread4 = spread_z(4)
    skew = send_mlp(4, 6, quarter(0), 1, along_y(1))
    skew += send_mlp(4, 6, quarter(0) + 1, 1, along_y(-1))
    mates = send_mlp(4, 5, quarter(0), 2, other_core())
    get_up.wait()
    get_down.wait()
    beside = send_mlp(0, 2, 0, 4, along_y(1))
    beside += send_mlp(0, 2, 4, 4, along_y(-1))
    mates_low = send_mlp(0, 1, 0, 8, other_core())
    onward = []
    source = lax.rem(row, 8) // 4 * 64 + row // 8 * 4 + lax.rem(row, 4)
    order = jnp.where(col == source, 1.0, 0.0).astype(BF)
    blocks[0] = dot(order, back[...]).astype(BF)

    def attend(b):
        both = jnp.concatenate([blocks[b], others[b]], 0)
        qkv4[...] = dot(both, wa[...]).astype(BF)
        outs = []
        for pair in range(2):
            normed = []
            for n in range(3):
                value = qkv4[:, pl.ds(768 * pair + 256 * n, 256)]
                full = value.astype(F32)
                full = full * inverse_norms(full, square)
                for i in range(2):
                    part_of = slice(128 * i, 128 * i + 128)
                    kind = (2 * n + i) % 3
                    normed.append(value[:, part_of] if kind == 2 else full[:, part_of])
            for s in range(2):
                q, k, v = normed[3 * s : 3 * s + 3]
                q = (q[:128] * tabs[2 * pair + s, 0, pl.ds(4, 1), pl.ds(0, 128)]).astype(BF)
                k = k.astype(BF)
                right = jnp.concatenate([v, jnp.ones((256, 128), BF)], 1)
                sums = []
                for h in range(3):
                    n = 3 * (2 * pair + s) + h
                    spot = jnp.concatenate(
                        [bias3[bias_rows(n, 0), :], bias3[bias_rows(n, 1), :]], 1
                    )
                    score = dot_nt(q * masks[h], k) + spot
                    sums.append(dot(jnp.exp(score).astype(BF), right))
                outs.append(
                    (
                        lane_pick([o[:, :128] for o in sums])
                        / lane_pick([o[:, 128:] for o in sums])
                    ).astype(BF)
                )
        part[b][...] = dot(jnp.concatenate(outs, 1), wp[...].reshape(512, 1536)).astype(BF)

    def ring(held, buf, compute, meet, after):
        right = w.go(held.at[0], held.at[1], along_x(1))
        left = w.go(held.at[0], held.at[2], along_x(-1))
        meet(0)
        compute(0)
        after(0)
        right.wait_recv()
        on_right = w.go(held.at[1, first], held.at[3, first], along_x(1))
        left.wait_recv()
        on_left = w.go(held.at[2, second], held.at[3, second], along_x(-1))
        meet(1)
        compute(1)
        near_left = w.go(part[1], buf.at[0], along_x(-1))
        after(1)
        meet(2)
        compute(2)
        near_right = w.go(part[2], buf.at[1], along_x(1))
        after(2)
        on_right.wait_recv()
        on_left.wait_recv()
        meet(3)
        compute(3)
        far = w.go(part[3], buf.at[2], along_x(2))
        after(3)
        total = part[0][...].astype(F32)
        near_left.wait_recv()
        near_right.wait_recv()
        total = total + buf[0].astype(F32) + buf[1].astype(F32)
        far.wait_recv()
        total = total + buf[2].astype(F32)
        for c in (right, left, on_right, on_left, near_left, near_right, far):
            c.wait_send()
        return total

    crossing = []

    def meet_core(b):
        if b == 0:
            crossing.append(w.go(blocks.at[0], others.at[0], other_core()))
            for flight in (flight_a, flight_p):
                flight[2].wait_recv()
            for c in late:
                c.wait_recv()
        if b == 1:
            crossing.append(w.go(blocks.at[1], others.at[1], other_core()))
            crossing.append(w.go(blocks.at[2], others.at[2], other_core()))
        if b == 3:
            crossing.append(w.go(blocks.at[3], others.at[3], other_core()))
        crossing[b].wait_recv()

    spread6 = []
    ends = []

    def after(b):
        if b == 0:
            arrive(skew)
            spread6.extend(spread_z(6))
            mates.extend(send_mlp(6, 7, quarter(0), 2, other_core()))
        if b == 1:
            a, c = forward_z(4, spread4)
            ends.append((4, a))
            mates.extend(c)
        if b == 3:
            a, c = forward_z(6, spread6)
            ends.append((6, a))
            mates.extend(c)
            arrive(beside)
            mates_low.extend(send_mlp(2, 3, 0, 8, other_core()))

    total = ring(blocks, buf4, attend, meet_core, after)
    total = layer_norm(total, gain_attn4[...].reshape(1, 1536))
    hidden[...] = (blocks[0].astype(F32) + total).astype(BF)

    visits = [
        w.go(hidden.at[first], visit.at[first], along_x(1)),
        w.go(hidden.at[second], visit.at[second], along_x(-1)),
    ]

    def units(tokens, half):
        return gelu(dot(tokens, wu[:, pl.ds(1536 * half, 1536)])).astype(BF)

    arrive(mates_low)
    own = dot(units(hidden[...], 0), wd[pl.ds(0, 1536), :])
    for slot, copies in ends:
        arrive(copies)
        mates.extend(send_mlp(slot, slot + 1, quarter(2), 2, other_core()))
    arrive(visits)
    guest = dot(units(visit[...], 0), wd[pl.ds(0, 1536), :])
    arrive(mates)
    inner = units(visit[...], 1)
    returns = []
    for n in range(2):
        cols = pl.ds(768 * n, 768)
        value = guest[:, 768 * n : 768 * n + 768] + dot(inner, wd[pl.ds(1536, 1536), cols])
        visit_part[:, cols] = value.astype(BF)
        returns += [
            w.go(visit_part.at[first, cols], bufm.at[first, cols], along_x(-1)),
            w.go(visit_part.at[second, cols], bufm.at[second, cols], along_x(1)),
        ]
    own = own + dot(units(hidden[...], 1), wd[pl.ds(1536, 1536), :])
    sent = halo + flight_t + crossing + late + across + skew + beside + mates + mates_low
    for f in spread4 + tuple(spread6) + flight_a + flight_p:
        sent += f if isinstance(f, list) else [f]
    for slot, copies in ends:
        sent += copies
    for c in sent + visits + returns:
        c.wait_send()
    arrive(returns)
    total = layer_norm(own + bufm[...].astype(F32), gain_mlp4[...].reshape(1, 1536))
    out_ref[...] = (hidden[...].astype(F32) + total).astype(BF).reshape(16, 8, 1536)


def per_device(
    tokens,
    regions,
    w_qkv3,
    w_proj3,
    bias_table3,
    logit_scale3,
    gain_attn3,
    w_merge,
    gain_merge,
    w_qkv4,
    w_proj4,
    bias_table4,
    logit_scale4,
    gain_attn4,
    w_up4,
    w_down4,
    gain_mlp4,
):
    any_ = pl.BlockSpec(memory_space=pl.ANY)
    vm = pl.BlockSpec(memory_space=pltpu.VMEM)
    sm = pl.BlockSpec(memory_space=pltpu.SMEM)
    out = pl.pallas_call(
        whole_kernel,
        name="whole",
        out_shape=jax.ShapeDtypeStruct((16, 8, 1536), BF),
        in_specs=[any_, vm, vm, vm, sm, sm, any_, any_, vm, any_, vm, any_, any_, vm, any_, any_, vm],
        out_specs=vm,
        scratch_shapes=[
            pltpu.VMEM((512, 768), BF),
            pltpu.VMEM((2, 256, 768), BF),
            pltpu.VMEM((2, 256, 768), BF),
            pltpu.VMEM((512, 128), BF),
            pltpu.VMEM((768, 2304), BF),
            pltpu.VMEM((768, 768), BF),
            pltpu.VMEM((3072, 1536), BF),
            pltpu.VMEM((18, 512, 128), BF),
            pltpu.VMEM((72 * 128, 128), F32),
            pltpu.VMEM((4, 3, 8, 256), F32),
            pltpu.VMEM((3, 96, 1536), BF),
            pltpu.VMEM((1536, 1536), BF),
            pltpu.VMEM((4, 128, 1536), BF),
            pltpu.VMEM((4, 128, 1536), BF),
            pltpu.VMEM((4, 128, 1536), BF),
            pltpu.VMEM((3, 128, 1536), BF),
            pltpu.VMEM((128, 1536), BF),
            pltpu.VMEM((1536, 3072), BF),
            pltpu.VMEM((3072, 1536), BF),
            pltpu.SemaphoreType.DMA((WIRES,)),
            pltpu.SemaphoreType.DMA((WIRES,)),
            pltpu.SemaphoreType.DMA((8,)),
        ],
        compiler_params=pltpu.CompilerParams(
            collective_id=1, has_side_effects=True, vmem_limit_bytes=VMEM_LIMIT
        ),
    )(
        tokens.reshape(512, 768),
        regions.T,
        bias_table3.transpose(1, 0, 2),
        bias_table4,
        logit_scale3,
        logit_scale4,
        w_qkv3,
        w_proj3,
        gain_attn3,
        w_merge,
        gain_merge,
        w_qkv4.transpose(0, 2, 1),
        w_proj4,
        gain_attn4,
        w_up4,
        w_down4,
        gain_mlp4,
    )
    return out

def solution(mesh):
    placed = (
        P("wide", "narrow", None),
        P("wide", "narrow"),
        P(),
        P(),
        P(),
        P(),
        P(),
        P(),
        P(),
        P(None, None, "narrow"),
        P("narrow", None),
        P("narrow", None, None),
        P("narrow"),
        P(),
        P(None, "narrow"),
        P("narrow", None),
        P(),
    )
    return jax.shard_map(
        per_device, mesh=mesh, in_specs=placed, out_specs=P("wide", "narrow", None), check_vma=False
    )
```

```python
import jax
import jax.numpy as jnp
from jax import lax
from jax.experimental import pallas as pl
from jax.experimental.pallas import tpu as pltpu
from jax.sharding import PartitionSpec as P

HD = 32
MESH = pl.DeviceIdType.MESH
BF = jnp.bfloat16
F32 = jnp.float32
MASK = 100.0
WIRES = 128
VMEM_LIMIT = 61 << 20


def place():
    wide, narrow = lax.axis_index("wide"), lax.axis_index("narrow")
    return wide, narrow


def shifted(dw, dn):
    wide, narrow = place()
    return (lax.rem(wide + dw + 8, 8), lax.rem(narrow + dn + 16, 16))


def along_x(step):
    wide, narrow = place()
    return (wide, lax.rem(narrow + 4 * step + 16, 16))


def along_y(step):
    wide, narrow = place()
    y = (wide // 4) * 2 + lax.rem(narrow // 2, 2)
    y = lax.rem(y + step + 4, 4)
    return (
        (y // 2) * 4 + lax.rem(wide, 4),
        (narrow // 4) * 4 + lax.rem(y, 2) * 2 + lax.rem(narrow, 2),
    )


def along_z(step):
    wide, narrow = place()
    return ((wide // 4) * 4 + lax.rem(wide + step + 4, 4), narrow)


def other_core():
    wide, narrow = place()
    return (wide, narrow + 1 - 2 * lax.rem(narrow, 2))


def quad(core, row):
    wide, narrow = place()
    c, r = lax.rem(narrow, 2), lax.rem(narrow // 2, 2)
    c = 1 - c if core else c
    r = 1 - r if row else r
    return (wide, (narrow // 4) * 4 + r * 2 + c)


def greet(sources, expected):
    barrier = pltpu.get_barrier_semaphore()
    for device in sources:
        pl.semaphore_signal(barrier, inc=1, device_id=device, device_id_type=MESH)
    pl.semaphore_wait(barrier, expected)


class Wires:
    def __init__(self, send, recv):
        self.send, self.recv, self.count = send, recv, 0

    def copy(self, src, dst, device):
        i = self.count
        self.count += 1
        out = pltpu.make_async_remote_copy(
            src_ref=src,
            dst_ref=dst,
            send_sem=self.send.at[i],
            recv_sem=self.recv.at[i],
            device_id=device,
            device_id_type=MESH,
        )
        return out

    def go(self, src, dst, device):
        out = self.copy(src, dst, device)
        out.start()
        return out


def dot(a, b):
    return jnp.dot(a, b, preferred_element_type=F32)


def dot_nt(a, b):
    return lax.dot_general(a, b, (((1,), (1,)), ((), ())), preferred_element_type=F32)


def iota(shape, axis):
    return lax.broadcasted_iota(jnp.int32, shape, axis)


def layer_norm(values, gain):
    center = jnp.mean(values, -1, keepdims=True)
    offset = values - center
    spread = jnp.mean(offset * offset, -1, keepdims=True)
    return offset * lax.rsqrt(spread + 1e-05) * gain


def gelu(x):
    return 0.5 * x * (1.0 + lax.erf(x * (2.0**-0.5)))


def head_blocks():
    same = iota((256, 256), 0) // HD == iota((256, 256), 1) // HD
    return jnp.where(same, 1.0, 0.0).astype(BF)


def inverse_norms(values, blocks):
    return lax.rsqrt(dot((values * values).astype(BF), blocks) + 1e-06)


def lane_pick(values):
    lane = iota((1, 128), 1)
    out = values[0]
    for h in range(1, len(values)):
        out = jnp.where(lane >= h * HD, values[h], out)
    return out


def head_masks(count):
    lane = iota((1, 128), 1) // HD
    return [jnp.where(lane == h, 1.0, 0.0).astype(BF) for h in range(count)]


def table_rows(logits, each):
    lane = iota((31, 1024), 1)
    column = 31 - 8 * (lane // 256) - lax.rem(lane, 8)
    pick = jnp.where(iota((31, 1024), 0) == column, 1.0, 0.0).astype(BF)
    high = logits.astype(BF)
    low = (logits - high.astype(F32)).astype(BF)
    moved = dot(high, pick) + dot(low, pick)
    row = iota(moved.shape, 0) // each
    f = lax.rem(iota(moved.shape, 1), 256) // 8
    moved = jnp.where(row == 30 - f, moved, 0.0)
    if each == 1:
        values = jnp.sum(moved, 0, keepdims=True)
    else:
        values = jnp.sum(moved.reshape(31, each, 1024), 0)
    return 16.0 / (1.0 + jnp.exp(-values))


def bias_tables(rows):
    sub = iota((8, 256), 0)
    lane = lax.rem(iota((8, 256), 1), 8)
    spread = [jnp.broadcast_to(r, (8, 256)) for r in rows]
    tables = []
    for m in range(1, 4):
        straight = pltpu.roll(spread[m], 0, 1, stride=1, stride_axis=0)
        around = pltpu.roll(spread[m - 1], 248, 1, stride=1, stride_axis=0)
        tables.append(jnp.where(lane >= sub, straight, around))
    return tables


def bias_block(table, a):
    return pltpu.roll(table, (256 - 8 * (15 - a)) % 256, 1)[:, :128]


def whole_kernel(
    tokens_ref,
    labels_ref,
    table3_ref,
    table4_ref,
    scale3_ref,
    scale4_ref,
    wqkv3_hbm,
    wproj3_hbm,
    gain_attn3,
    wm_hbm,
    gain_merge,
    wqkv4_hbm,
    wproj4_hbm,
    gain_attn4,
    wup_hbm,
    wdown_hbm,
    gain_mlp4,
    out_ref,
    ctx,
    xs,
    xr,
    aug,
    wqkv,
    wproj,
    wm,
    qkv,
    bias3,
    tabs,
    wtmp,
    wa,
    wp,
    blocks,
    others,
    buf4,
    visit,
    wu,
    wd,
    send,
    recv,
    local,
):
    w = Wires(send, recv)
    core = lax.rem(lax.axis_index("narrow"), 2)
    first, second = pl.ds(0, 64), pl.ds(64, 64)
    part = [wqkv.at[pl.ds(128 * b, 128), pl.ds(0, 1536)] for b in range(4)]
    qkv4 = wqkv.at[pl.ds(512, 256), pl.ds(0, 1536)]
    visit_part = part[0]
    back, hidden, bufm = visit, others.at[0], buf4.at[2]

    def bias_rows(n, t, start=0, size=128):
        return pl.ds(pl.multiple_of((3 * n + t) * 128 + start, 8), size)

    loads = []
    for i, (src, dst) in enumerate(
        (
            (tokens_ref, ctx),
            (wqkv4_hbm, wtmp),
            (wproj4_hbm, wp.at[0, pl.ds(0, 96)]),
            (wqkv3_hbm, wqkv),
            (wproj3_hbm, wproj),
            (wm_hbm, wm),
            (wup_hbm, wu.at[:, pl.ds(0, 384)]),
            (wdown_hbm, wd.at[pl.ds(0, 384)]),
        )
    ):
        load = pltpu.make_async_copy(src, dst, local.at[i])
        load.start()
        loads.append(load)
    get_tokens, get_qkv4, get_proj4, get_qkv3, get_proj3, get_merge, get_up, get_down = loads

    partners = [shifted(i, j) for i, j in ((0, 1), (1, 0), (1, 1), (0, -1), (-1, 0), (-1, -1))]
    partners += [quad(1, 0), quad(0, 1), quad(1, 1), along_x(1), along_x(-1), along_x(2)]
    partners += [along_y(1), along_y(-1), along_z(1), along_z(-1)]
    greet(partners, len(partners))

    get_tokens.wait()
    grouped = ctx[...].astype(F32).reshape(32, 2, 8, 768)
    for half in range(2):
        xs[half] = grouped[:, half].reshape(256, 768).astype(BF)
    halo = [
        w.go(xs.at[0, pl.ds(64, 192)], xr.at[1, pl.ds(0, 192)], shifted(0, -1)),
        w.go(xs.at[1, pl.ds(0, 64)], xr.at[0, pl.ds(192, 64)], shifted(-1, 0)),
        w.go(xs.at[0, pl.ds(0, 64)], xr.at[1, pl.ds(192, 64)], shifted(-1, -1)),
    ]
    xr[0, pl.ds(0, 192), :] = xs[1, pl.ds(64, 192), :]

    get_qkv4.wait()
    for j in range(3):
        wide = jnp.concatenate([wtmp[j].astype(F32), jnp.zeros((32, 1536), F32)], 0)
        wa[:, pl.ds(128 * j, 128)] = wide.T.astype(BF)
    get_proj4.wait()
    for s in range(4):
        wp[s, pl.ds(96, 32), :] = jnp.zeros((32, 1536), BF)

    def column(s):
        return pl.ds(384 * s, 384)

    def both_ways(own, away, cut):
        up, down = pl.ds(0, cut), pl.ds(cut, cut)
        return (
            w.go(own(0, up), away(2, up), along_y(1)),
            w.go(own(0, down), away(2, down), along_y(-1)),
            w.go(own(0, pl.ds(0, 2 * cut)), away(1, pl.ds(0, 2 * cut)), other_core()),
        )

    def pass_on(piece, cut, flight):
        up, down = pl.ds(0, cut), pl.ds(cut, cut)
        flight[0].wait_recv()
        a = w.go(piece(2, up), piece(3, up), other_core())
        flight[1].wait_recv()
        b = w.go(piece(2, down), piece(3, down), other_core())
        return a, b

    def piece_a(s, rows):
        return wa.at[rows, column(s)]

    def piece_p(s, rows):
        return wp.at[s, rows]

    plane = lax.rem(lax.axis_index("wide"), 4)

    def eighths(slot, start, count):
        down = pl.multiple_of(48 * start, 48)
        if slot is None:
            return (
                wup_hbm.at[pl.ds(pl.multiple_of(192 * start, 192), 192 * count)],
                wdown_hbm.at[pl.ds(down, 48 * count)],
            )
        return (
            wu.at[pl.ds(pl.multiple_of(192 * start, 192), 192 * count), column(slot)],
            wd.at[pl.ds(384 * slot + down, 48 * count)],
        )

    def send_mlp(source, target, start, count, device):
        return [
            w.go(a, b, device)
            for a, b in zip(eighths(source, start, count), eighths(target, start, count))
        ]

    def arrive(copies):
        for c in copies:
            c.wait_recv()

    def quarter(step):
        return 2 * lax.rem(plane + step + 4, 4)

    def spread_z(slot):
        return (
            send_mlp(slot, slot, quarter(0), 2, along_z(1)),
            send_mlp(slot, slot, quarter(0), 2, along_z(-1)),
        )

    def forward_z(slot, flight):
        arrive(flight[0])
        a = send_mlp(slot, slot, quarter(-1), 1, along_z(1))
        arrive(flight[1])
        b = send_mlp(slot, slot, quarter(1) + 1, 1, along_z(-1))
        c = send_mlp(slot, slot + 1, quarter(-1), 2, other_core())
        c += send_mlp(slot, slot + 1, quarter(1), 2, other_core())
        return a + b, c

    lane = iota((1, 256), 1)
    for h in range(3):
        row = table_rows(table4_ref[h], 1)
        for m in range(4):
            tabs[0, h, pl.ds(m, 1), :] = row[:, 256 * m : 256 * m + 256]
    tabs[0, 0, pl.ds(4, 1), :] = jnp.where(
        lane < HD, scale4_ref[0], jnp.where(lane < 2 * HD, scale4_ref[1], scale4_ref[2])
    )
    flight_t = [
        w.go(tabs.at[0], tabs.at[1], quad(1, 0)),
        w.go(tabs.at[0], tabs.at[2], quad(0, 1)),
        w.go(tabs.at[0], tabs.at[3], quad(1, 1)),
    ]

    token = iota((512, 16), 0)
    pick = token // 256 * 8 + lax.rem(token, 8) == iota((512, 16), 1)
    labels = dot(jnp.where(pick, 1.0, 0.0).astype(BF), labels_ref[...].astype(F32).astype(BF))
    pick = lax.rem(iota((512, 32), 0), 256) // 8 == iota((512, 32), 1)
    labels = jnp.where(pick, labels, 0.0).astype(BF)
    at = iota((512, 128), 1)
    labels = dot(labels, jnp.ones((32, 128), BF))
    aug[...] = jnp.where((labels == at.astype(F32)) | (at == 64), 1.0, 0.0).astype(BF)


    def build3(i, carry):
        heads = pl.ds(pl.multiple_of(8 * i, 8), 8)
        values = table_rows(table3_ref[:, heads, :].reshape(248, 31), 8)
        for h in range(8):
            tables = bias_tables([values[h : h + 1, 256 * m : 256 * m + 256] for m in range(4)])
            for t in range(3):
                for a in range(16):
                    bias3[bias_rows(8 * i + h, t, 8 * a, 8), :] = bias_block(tables[t], a)
        return carry

    lax.fori_loop(0, 3, build3, 0)

    flight_a = both_ways(piece_a, piece_a, 768)
    flight_p = both_ways(piece_p, piece_p, 48)

    get_qkv3.wait()
    for c in halo:
        c.wait_recv()
    across = send_mlp(None, 4, quarter(0), 2, along_x(2))
    x = xr[...].reshape(512, 768)
    square = head_blocks()
    lane = iota((1, 256), 1) // HD
    for j in range(3):
        out = dot(x, wqkv[:, pl.ds(768 * j, 768)]).astype(BF)
        for n in range(3):
            value = out[:, 256 * n : 256 * n + 256]
            if j < 2:
                value = value.astype(F32)
                factor = inverse_norms(value, square)
                if j == 0:
                    row = jnp.zeros((1, 256), F32)
                    for h in range(8):
                        row = jnp.where(lane == h, scale3_ref[8 * n + h], row)
                    factor = factor * row
                value = (value * factor).astype(BF)
            qkv[6 * j + 2 * n] = value[:, :128]
            qkv[6 * j + 2 * n + 1] = value[:, 128:]

    masks = head_masks(4)
    lane = iota((1, 128), 1)
    level = jnp.where(lane < 64, MASK, -MASK).astype(BF)

    def group(g, carry):
        for win in range(2):

            def rows(ref_at):
                return jnp.concatenate(
                    [ref_at(pl.ds(128 * win, 128)), ref_at(pl.ds(256 + 128 * win, 128))], 0
                )

            q, k, v = (rows(lambda r, j=j: qkv[6 * j + g, r, :]) for j in range(3))
            marks = rows(lambda r: aug[r, :])
            keys = jnp.concatenate([k, marks], 1)
            marks = marks * level
            right = jnp.concatenate([v, jnp.ones((256, 128), BF)], 1)
            outs = []
            for h in range(4):
                score = dot_nt(jnp.concatenate([q * masks[h], marks], 1), keys)
                side = [bias3[bias_rows(4 * g + h, t), :] for t in range(3)]
                spot = jnp.concatenate(
                    [
                        jnp.concatenate([side[1], side[2]], 1),
                        jnp.concatenate([side[0], side[1]], 1),
                    ],
                    0,
                )
                outs.append(dot(jnp.exp(score + spot).astype(BF), right))
            out = lane_pick([o[:, :128] for o in outs]) / lane_pick([o[:, 128:] for o in outs])
            out = out.astype(BF)
            cols = pl.ds(pl.multiple_of(g * 128, 128), 128)
            ctx[pl.ds(128 * win, 128), cols] = out[:128]
            ctx[pl.ds(256 + 128 * win, 128), cols] = out[128:]
        return carry

    lax.fori_loop(0, 6, group, 0, unroll=2)

    get_proj3.wait()
    y = dot(ctx[...], wproj[...])
    y = layer_norm(y, gain_attn3[...].reshape(1, 768)) + x.astype(F32)
    y = y.astype(BF).astype(F32)
    for half in range(2):
        for r in range(32):
            source = half * 256 + 8 * r
            for m in range(6):
                bias3[pl.ds(512 * m + r * 16 + half * 8, 8), :] = y[
                    source : source + 8, 128 * m : 128 * m + 128
                ]
    pieces = []
    for j in range(2):
        side = jnp.concatenate(
            [bias3[pl.ds(512 * m + j, 256, stride=2), :] for m in range(6)], 1
        ).reshape(16, 2, 8, 768)
        for i in range(2):
            pieces.append(side[:, i].reshape(128, 768).astype(BF))
    get_merge.wait()
    merged = dot(jnp.concatenate(pieces, 1), wm[...])
    merged = layer_norm(merged, gain_merge[...].reshape(1, 1536)).astype(BF)
    row, col = iota((128, 128), 0), iota((128, 128), 1)
    source = lax.rem(row, 64) // 4 * 8 + row // 64 * 4 + lax.rem(row, 4)
    order = jnp.where(col == source, 1.0, 0.0).astype(BF)
    m4 = part[0]
    m4[...] = dot(order, merged).astype(BF)

    shift = [
        w.go(m4.at[pl.ds(64, 48)], back.at[pl.ds(16, 48)], shifted(0, 1)),
        w.go(m4.at[pl.ds(48, 16)], back.at[pl.ds(64, 16)], shifted(1, 0)),
        w.go(m4.at[pl.ds(112, 16)], back.at[pl.ds(0, 16)], shifted(1, 1)),
    ]
    back[pl.ds(80, 48), :] = m4[pl.ds(0, 48), :]
    for c in flight_t:
        c.wait_recv()

    def build4(n, carry):
        s, h = n // 3, lax.rem(n, 3)
        rows = tabs[s, h]
        tables = bias_tables([rows[m : m + 1] for m in range(4)])
        side = jnp.where(core == 0, tables[2], tables[0])
        for a in range(16):
            bias3[bias_rows(n, 0, 8 * a, 8), :] = bias_block(tables[1], a)
            bias3[bias_rows(n, 1, 8 * a, 8), :] = bias_block(side, a)
        return carry

    lax.fori_loop(0, 12, build4, 0)
    for c in shift:
        c.wait()
    source = lax.rem(row, 8) // 4 * 64 + row // 8 * 4 + lax.rem(row, 4)
    order = jnp.where(col == source, 1.0, 0.0).astype(BF)
    blocks[0] = dot(order, back[...]).astype(BF)
    right = w.go(blocks.at[0], blocks.at[1], along_x(1))
    left = w.go(blocks.at[0], blocks.at[2], along_x(-1))
    crossing = [w.go(blocks.at[0], others.at[0], other_core())]

    late = list(pass_on(piece_a, 768, flight_a) + pass_on(piece_p, 48, flight_p))
    arrive(across)
    spread4 = spread_z(4)
    skew = send_mlp(4, 6, quarter(0), 1, along_y(1))
    skew += send_mlp(4, 6, quarter(0) + 1, 1, along_y(-1))
    mates = send_mlp(4, 5, quarter(0), 2, other_core())
    get_up.wait()
    get_down.wait()
    mates_low = send_mlp(0, 1, 0, 8, other_core())
    beside, spread6, ends = [], [], []

    def attend(b):
        both = jnp.concatenate([blocks[b], others[b]], 0)
        qkv4[...] = dot(both, wa[...]).astype(BF)
        outs = []
        for pair in range(2):
            normed = []
            for n in range(3):
                value = qkv4[:, pl.ds(768 * pair + 256 * n, 256)]
                full = value.astype(F32)
                full = full * inverse_norms(full, square)
                for i in range(2):
                    part_of = slice(128 * i, 128 * i + 128)
                    kind = (2 * n + i) % 3
                    normed.append(value[:, part_of] if kind == 2 else full[:, part_of])
            for s in range(2):
                q, k, v = normed[3 * s : 3 * s + 3]
                q = (q[:128] * tabs[2 * pair + s, 0, pl.ds(4, 1), pl.ds(0, 128)]).astype(BF)
                k = k.astype(BF)
                right = jnp.concatenate([v, jnp.ones((256, 128), BF)], 1)
                sums = []
                for h in range(3):
                    n = 3 * (2 * pair + s) + h
                    spot = jnp.concatenate(
                        [bias3[bias_rows(n, 0), :], bias3[bias_rows(n, 1), :]], 1
                    )
                    score = dot_nt(q * masks[h], k) + spot
                    sums.append(dot(jnp.exp(score).astype(BF), right))
                outs.append(
                    (
                        lane_pick([o[:, :128] for o in sums])
                        / lane_pick([o[:, 128:] for o in sums])
                    ).astype(BF)
                )
        part[b][...] = dot(jnp.concatenate(outs, 1), wp[...].reshape(512, 1536)).astype(BF)

    for flight in (flight_a, flight_p):
        flight[2].wait_recv()
    arrive(late)
    crossing[0].wait_recv()
    attend(0)
    beside += send_mlp(0, 2, 0, 4, along_y(1))
    beside += send_mlp(0, 2, 4, 4, along_y(-1))
    right.wait_recv()
    crossing.append(w.go(blocks.at[1], others.at[1], other_core()))
    on_right = w.go(blocks.at[1, first], blocks.at[3, first], along_x(1))
    left.wait_recv()
    crossing.append(w.go(blocks.at[2], others.at[2], other_core()))
    on_left = w.go(blocks.at[2, second], blocks.at[3, second], along_x(-1))
    crossing[1].wait_recv()
    attend(1)
    sums = [w.go(part[1].at[first], buf4.at[1, first], along_x(-1))]
    arrive(skew)
    spread6 += spread_z(6)
    mates += send_mlp(6, 7, quarter(0), 2, other_core())
    crossing[2].wait_recv()
    attend(2)
    sums.append(w.go(part[2].at[second], buf4.at[0, second], along_x(1)))
    on_right.wait_recv()
    crossing.append(w.go(blocks.at[3, first], others.at[3, first], other_core()))
    on_left.wait_recv()
    crossing.append(w.go(blocks.at[3, second], others.at[3, second], other_core()))
    crossing[3].wait_recv()
    crossing[4].wait_recv()
    attend(3)
    far_right = w.go(part[3].at[first], buf4.at[2, first], along_x(1))
    far_left = w.go(part[3].at[second], buf4.at[2, second], along_x(-1))
    far_right.wait_recv()
    part[2][first, :] = (part[2][first, :].astype(F32) + buf4[2, first, :].astype(F32)).astype(BF)
    sums.append(w.go(part[2].at[first], buf4.at[0, first], along_x(1)))
    far_left.wait_recv()
    part[1][second, :] = (
        part[1][second, :].astype(F32) + buf4[2, second, :].astype(F32)
    ).astype(BF)
    sums.append(w.go(part[1].at[second], buf4.at[1, second], along_x(-1)))
    for slot, flight in ((4, spread4), (6, spread6)):
        onward, copies = forward_z(slot, flight)
        ends.append((slot, onward))
        mates += copies
    arrive(beside)
    mates_low += send_mlp(2, 3, 0, 8, other_core())
    arrive(sums)
    total = part[0][...].astype(F32) + buf4[0].astype(F32) + buf4[1].astype(F32)
    for c in [right, left, on_right, on_left, far_right, far_left] + sums:
        c.wait_send()
    total = layer_norm(total, gain_attn4[...].reshape(1, 1536))
    hidden[...] = (blocks[0].astype(F32) + total).astype(BF)

    visits = [
        w.go(hidden.at[first], visit.at[first], along_x(1)),
        w.go(hidden.at[second], visit.at[second], along_x(-1)),
    ]

    def units(tokens, half):
        return gelu(dot(tokens, wu[:, pl.ds(1536 * half, 1536)])).astype(BF)

    arrive(mates_low)
    own = dot(units(hidden[...], 0), wd[pl.ds(0, 1536), :])
    for slot, copies in ends:
        arrive(copies)
        mates.extend(send_mlp(slot, slot + 1, quarter(2), 2, other_core()))
    arrive(visits)
    guest = dot(units(visit[...], 0), wd[pl.ds(0, 1536), :])
    arrive(mates)
    inner = units(visit[...], 1)
    returns = []
    for n in range(2):
        cols = pl.ds(768 * n, 768)
        value = guest[:, 768 * n : 768 * n + 768] + dot(inner, wd[pl.ds(1536, 1536), cols])
        visit_part[:, cols] = value.astype(BF)
        returns += [
            w.go(visit_part.at[first, cols], bufm.at[first, cols], along_x(-1)),
            w.go(visit_part.at[second, cols], bufm.at[second, cols], along_x(1)),
        ]
    own = own + dot(units(hidden[...], 1), wd[pl.ds(1536, 1536), :])
    sent = halo + flight_t + crossing + late + across + skew + beside + mates + mates_low
    for f in spread4 + tuple(spread6) + flight_a + flight_p:
        sent += f if isinstance(f, list) else [f]
    for slot, copies in ends:
        sent += copies
    for c in sent + visits + returns:
        c.wait_send()
    arrive(returns)
    total = layer_norm(own + bufm[...].astype(F32), gain_mlp4[...].reshape(1, 1536))
    out_ref[...] = (hidden[...].astype(F32) + total).astype(BF).reshape(16, 8, 1536)


def per_device(
    tokens,
    regions,
    w_qkv3,
    w_proj3,
    bias_table3,
    logit_scale3,
    gain_attn3,
    w_merge,
    gain_merge,
    w_qkv4,
    w_proj4,
    bias_table4,
    logit_scale4,
    gain_attn4,
    w_up4,
    w_down4,
    gain_mlp4,
):
    any_ = pl.BlockSpec(memory_space=pl.ANY)
    vm = pl.BlockSpec(memory_space=pltpu.VMEM)
    sm = pl.BlockSpec(memory_space=pltpu.SMEM)
    out = pl.pallas_call(
        whole_kernel,
        name="whole",
        out_shape=jax.ShapeDtypeStruct((16, 8, 1536), BF),
        in_specs=[any_, vm, vm, vm, sm, sm, any_, any_, vm, any_, vm, any_, any_, vm, any_, any_, vm],
        out_specs=vm,
        scratch_shapes=[
            pltpu.VMEM((512, 768), BF),
            pltpu.VMEM((2, 256, 768), BF),
            pltpu.VMEM((2, 256, 768), BF),
            pltpu.VMEM((512, 128), BF),
            pltpu.VMEM((768, 2304), BF),
            pltpu.VMEM((768, 768), BF),
            pltpu.VMEM((3072, 1536), BF),
            pltpu.VMEM((18, 512, 128), BF),
            pltpu.VMEM((72 * 128, 128), F32),
            pltpu.VMEM((4, 3, 8, 256), F32),
            pltpu.VMEM((3, 96, 1536), BF),
            pltpu.VMEM((1536, 1536), BF),
            pltpu.VMEM((4, 128, 1536), BF),
            pltpu.VMEM((4, 128, 1536), BF),
            pltpu.VMEM((4, 128, 1536), BF),
            pltpu.VMEM((3, 128, 1536), BF),
            pltpu.VMEM((128, 1536), BF),
            pltpu.VMEM((1536, 3072), BF),
            pltpu.VMEM((3072, 1536), BF),
            pltpu.SemaphoreType.DMA((WIRES,)),
            pltpu.SemaphoreType.DMA((WIRES,)),
            pltpu.SemaphoreType.DMA((8,)),
        ],
        compiler_params=pltpu.CompilerParams(
            collective_id=1, has_side_effects=True, vmem_limit_bytes=VMEM_LIMIT
        ),
    )(
        tokens.reshape(512, 768),
        regions.T,
        bias_table3.transpose(1, 0, 2),
        bias_table4,
        logit_scale3,
        logit_scale4,
        w_qkv3,
        w_proj3,
        gain_attn3,
        w_merge,
        gain_merge,
        w_qkv4.transpose(0, 2, 1),
        w_proj4,
        gain_attn4,
        w_up4,
        w_down4,
        gain_mlp4,
    )
    return out

def solution(mesh):
    placed = (
        P("wide", "narrow", None),
        P("wide", "narrow"),
        P(),
        P(),
        P(),
        P(),
        P(),
        P(),
        P(),
        P(None, None, "narrow"),
        P("narrow", None),
        P("narrow", None, None),
        P("narrow"),
        P(),
        P(None, "narrow"),
        P("narrow", None),
        P(),
    )
    return jax.shard_map(
        per_device, mesh=mesh, in_specs=placed, out_specs=P("wide", "narrow", None), check_vma=False
    )
```

```python
import jax
import jax.numpy as jnp
from jax import lax
from jax.experimental import pallas as pl
from jax.experimental.pallas import tpu as pltpu
from jax.sharding import PartitionSpec as P

HD = 32
MESH = pl.DeviceIdType.MESH
BF = jnp.bfloat16
F32 = jnp.float32
MASK = 100.0
WIRES = 128
VMEM_LIMIT = 61 << 20


def place():
    wide, narrow = lax.axis_index("wide"), lax.axis_index("narrow")
    return wide, narrow


def shifted(dw, dn):
    wide, narrow = place()
    return (lax.rem(wide + dw + 8, 8), lax.rem(narrow + dn + 16, 16))


def along_x(step):
    wide, narrow = place()
    return (wide, lax.rem(narrow + 4 * step + 16, 16))


def along_y(step):
    wide, narrow = place()
    y = (wide // 4) * 2 + lax.rem(narrow // 2, 2)
    y = lax.rem(y + step + 4, 4)
    return (
        (y // 2) * 4 + lax.rem(wide, 4),
        (narrow // 4) * 4 + lax.rem(y, 2) * 2 + lax.rem(narrow, 2),
    )


def along_z(step):
    wide, narrow = place()
    return ((wide // 4) * 4 + lax.rem(wide + step + 4, 4), narrow)


def other_core():
    wide, narrow = place()
    return (wide, narrow + 1 - 2 * lax.rem(narrow, 2))


def quad(core, row):
    wide, narrow = place()
    c, r = lax.rem(narrow, 2), lax.rem(narrow // 2, 2)
    c = 1 - c if core else c
    r = 1 - r if row else r
    return (wide, (narrow // 4) * 4 + r * 2 + c)


def greet(sources, expected):
    barrier = pltpu.get_barrier_semaphore()
    for device in sources:
        pl.semaphore_signal(barrier, inc=1, device_id=device, device_id_type=MESH)
    pl.semaphore_wait(barrier, expected)


class Wires:
    def __init__(self, send, recv):
        self.send, self.recv, self.count = send, recv, 0

    def copy(self, src, dst, device):
        i = self.count
        self.count += 1
        out = pltpu.make_async_remote_copy(
            src_ref=src,
            dst_ref=dst,
            send_sem=self.send.at[i],
            recv_sem=self.recv.at[i],
            device_id=device,
            device_id_type=MESH,
        )
        return out

    def go(self, src, dst, device):
        out = self.copy(src, dst, device)
        out.start()
        return out


def dot(a, b):
    return jnp.dot(a, b, preferred_element_type=F32)


def dot_nt(a, b):
    return lax.dot_general(a, b, (((1,), (1,)), ((), ())), preferred_element_type=F32)


def iota(shape, axis):
    return lax.broadcasted_iota(jnp.int32, shape, axis)


def layer_norm(values, gain):
    center = jnp.mean(values, -1, keepdims=True)
    offset = values - center
    spread = jnp.mean(offset * offset, -1, keepdims=True)
    return offset * lax.rsqrt(spread + 1e-05) * gain


def gelu(x):
    return 0.5 * x * (1.0 + lax.erf(x * (2.0**-0.5)))


def head_blocks():
    same = iota((256, 256), 0) // HD == iota((256, 256), 1) // HD
    return jnp.where(same, 1.0, 0.0).astype(BF)


def inverse_norms(values, blocks):
    return lax.rsqrt(dot((values * values).astype(BF), blocks) + 1e-06)


def lane_pick(values):
    lane = iota((1, 128), 1)
    out = values[0]
    for h in range(1, len(values)):
        out = jnp.where(lane >= h * HD, values[h], out)
    return out


def head_masks(count):
    lane = iota((1, 128), 1) // HD
    return [jnp.where(lane == h, 1.0, 0.0).astype(BF) for h in range(count)]


def table_rows(logits, each):
    lane = iota((31, 1024), 1)
    column = 31 - 8 * (lane // 256) - lax.rem(lane, 8)
    pick = jnp.where(iota((31, 1024), 0) == column, 1.0, 0.0).astype(BF)
    high = logits.astype(BF)
    low = (logits - high.astype(F32)).astype(BF)
    moved = dot(high, pick) + dot(low, pick)
    row = iota(moved.shape, 0) // each
    f = lax.rem(iota(moved.shape, 1), 256) // 8
    moved = jnp.where(row == 30 - f, moved, 0.0)
    if each == 1:
        values = jnp.sum(moved, 0, keepdims=True)
    else:
        values = jnp.sum(moved.reshape(31, each, 1024), 0)
    return 16.0 / (1.0 + jnp.exp(-values))


def bias_tables(rows):
    sub = iota((8, 256), 0)
    lane = lax.rem(iota((8, 256), 1), 8)
    spread = [jnp.broadcast_to(r, (8, 256)) for r in rows]
    tables = []
    for m in range(1, 4):
        straight = pltpu.roll(spread[m], 0, 1, stride=1, stride_axis=0)
        around = pltpu.roll(spread[m - 1], 248, 1, stride=1, stride_axis=0)
        tables.append(jnp.where(lane >= sub, straight, around))
    return tables


def bias_block(table, a):
    far = 8 * (15 - a)
    if far == 0:
        return table[:, :128]
    mixed = jnp.where(iota((8, 128), 1) >= far, table[:, :128], table[:, 128:])
    return pltpu.roll(mixed, 128 - far, 1)


def whole_kernel(
    tokens_ref,
    labels_ref,
    table3_ref,
    table4_ref,
    scale3_ref,
    scale4_ref,
    wqkv3_hbm,
    wproj3_hbm,
    gain_attn3,
    wm_hbm,
    gain_merge,
    wqkv4_hbm,
    wproj4_hbm,
    gain_attn4,
    wup_hbm,
    wdown_hbm,
    gain_mlp4,
    out_ref,
    ctx,
    xs,
    xr,
    aug,
    wqkv,
    wproj,
    wm,
    qkv,
    bias3,
    tabs,
    wtmp,
    wa,
    wp,
    blocks,
    others,
    buf4,
    visit,
    wu,
    wd,
    send,
    recv,
    local,
):
    w = Wires(send, recv)
    core = lax.rem(lax.axis_index("narrow"), 2)
    first, second = pl.ds(0, 64), pl.ds(64, 64)
    part = [wqkv.at[pl.ds(128 * b, 128), pl.ds(0, 1536)] for b in range(4)]
    qkv4 = wqkv.at[pl.ds(512, 256), pl.ds(0, 1536)]
    visit_part = part[0]
    back, hidden, bufm = visit, others.at[0], buf4.at[2]

    def bias_rows(n, t, start=0, size=128):
        return pl.ds(pl.multiple_of((3 * n + t) * 128 + start, 8), size)

    loads = []
    for i, (src, dst) in enumerate(
        (
            (tokens_ref, ctx),
            (wqkv4_hbm, wtmp),
            (wproj4_hbm, wp.at[0, pl.ds(0, 96)]),
            (wqkv3_hbm, wqkv),
            (wproj3_hbm, wproj),
            (wm_hbm, wm),
            (wup_hbm, wu.at[:, pl.ds(0, 384)]),
            (wdown_hbm, wd.at[pl.ds(0, 384)]),
        )
    ):
        load = pltpu.make_async_copy(src, dst, local.at[i])
        load.start()
        loads.append(load)
    get_tokens, get_qkv4, get_proj4, get_qkv3, get_proj3, get_merge, get_up, get_down = loads

    partners = [shifted(i, j) for i, j in ((0, 1), (1, 0), (1, 1), (0, -1), (-1, 0), (-1, -1))]
    partners += [quad(1, 0), quad(0, 1), quad(1, 1), along_x(1), along_x(-1), along_x(2)]
    partners += [along_y(1), along_y(-1), along_z(1), along_z(-1)]
    greet(partners, len(partners))

    get_tokens.wait()
    grouped = ctx[...].astype(F32).reshape(32, 2, 8, 768)
    for half in range(2):
        xs[half] = grouped[:, half].reshape(256, 768).astype(BF)
    halo = [
        w.go(xs.at[0, pl.ds(64, 192)], xr.at[1, pl.ds(0, 192)], shifted(0, -1)),
        w.go(xs.at[1, pl.ds(0, 64)], xr.at[0, pl.ds(192, 64)], shifted(-1, 0)),
        w.go(xs.at[0, pl.ds(0, 64)], xr.at[1, pl.ds(192, 64)], shifted(-1, -1)),
    ]
    xr[0, pl.ds(0, 192), :] = xs[1, pl.ds(64, 192), :]

    get_qkv4.wait()
    for j in range(3):
        wide = jnp.concatenate([wtmp[j].astype(F32), jnp.zeros((32, 1536), F32)], 0)
        wa[:, pl.ds(128 * j, 128)] = wide.T.astype(BF)
    get_proj4.wait()
    for s in range(4):
        wp[s, pl.ds(96, 32), :] = jnp.zeros((32, 1536), BF)

    def column(s):
        return pl.ds(384 * s, 384)

    def both_ways(own, away, cut):
        up, down = pl.ds(0, cut), pl.ds(cut, cut)
        return (
            w.go(own(0, up), away(2, up), along_y(1)),
            w.go(own(0, down), away(2, down), along_y(-1)),
            w.go(own(0, pl.ds(0, 2 * cut)), away(1, pl.ds(0, 2 * cut)), other_core()),
        )

    def pass_on(piece, cut, flight):
        up, down = pl.ds(0, cut), pl.ds(cut, cut)
        flight[0].wait_recv()
        a = w.go(piece(2, up), piece(3, up), other_core())
        flight[1].wait_recv()
        b = w.go(piece(2, down), piece(3, down), other_core())
        return a, b

    def piece_a(s, rows):
        return wa.at[rows, column(s)]

    def piece_p(s, rows):
        return wp.at[s, rows]

    plane = lax.rem(lax.axis_index("wide"), 4)

    def eighths(slot, start, count):
        down = pl.multiple_of(48 * start, 48)
        if slot is None:
            return (
                wup_hbm.at[pl.ds(pl.multiple_of(192 * start, 192), 192 * count)],
                wdown_hbm.at[pl.ds(down, 48 * count)],
            )
        return (
            wu.at[pl.ds(pl.multiple_of(192 * start, 192), 192 * count), column(slot)],
            wd.at[pl.ds(384 * slot + down, 48 * count)],
        )

    def send_mlp(source, target, start, count, device):
        return [
            w.go(a, b, device)
            for a, b in zip(eighths(source, start, count), eighths(target, start, count))
        ]

    def arrive(copies):
        for c in copies:
            c.wait_recv()

    def quarter(step):
        return 2 * lax.rem(plane + step + 4, 4)

    def spread_z(slot):
        return (
            send_mlp(slot, slot, quarter(0), 2, along_z(1)),
            send_mlp(slot, slot, quarter(0), 2, along_z(-1)),
        )

    def forward_z(slot, flight):
        arrive(flight[0])
        a = send_mlp(slot, slot, quarter(-1), 1, along_z(1))
        arrive(flight[1])
        b = send_mlp(slot, slot, quarter(1) + 1, 1, along_z(-1))
        c = send_mlp(slot, slot + 1, quarter(-1), 2, other_core())
        c += send_mlp(slot, slot + 1, quarter(1), 2, other_core())
        return a + b, c

    lane = iota((1, 256), 1)
    for h in range(3):
        row = table_rows(table4_ref[h], 1)
        for m in range(4):
            tabs[0, h, pl.ds(m, 1), :] = row[:, 256 * m : 256 * m + 256]
    tabs[0, 0, pl.ds(4, 1), :] = jnp.where(
        lane < HD, scale4_ref[0], jnp.where(lane < 2 * HD, scale4_ref[1], scale4_ref[2])
    )
    flight_t = [
        w.go(tabs.at[0], tabs.at[1], quad(1, 0)),
        w.go(tabs.at[0], tabs.at[2], quad(0, 1)),
        w.go(tabs.at[0], tabs.at[3], quad(1, 1)),
    ]

    token = iota((512, 16), 0)
    pick = token // 256 * 8 + lax.rem(token, 8) == iota((512, 16), 1)
    labels = dot(jnp.where(pick, 1.0, 0.0).astype(BF), labels_ref[...].astype(F32).astype(BF))
    pick = lax.rem(iota((512, 32), 0), 256) // 8 == iota((512, 32), 1)
    labels = jnp.where(pick, labels, 0.0).astype(BF)
    at = iota((512, 128), 1)
    labels = dot(labels, jnp.ones((32, 128), BF))
    aug[...] = jnp.where((labels == at.astype(F32)) | (at == 64), 1.0, 0.0).astype(BF)


    def build3(i, carry):
        heads = pl.ds(pl.multiple_of(8 * i, 8), 8)
        values = table_rows(table3_ref[:, heads, :].reshape(248, 31), 8)
        for h in range(8):
            tables = bias_tables([values[h : h + 1, 256 * m : 256 * m + 256] for m in range(4)])
            for t in range(3):
                for a in range(16):
                    bias3[bias_rows(8 * i + h, t, 8 * a, 8), :] = bias_block(tables[t], a)
        return carry

    lax.fori_loop(0, 3, build3, 0)

    flight_a = both_ways(piece_a, piece_a, 768)
    flight_p = both_ways(piece_p, piece_p, 48)

    get_qkv3.wait()
    for c in halo:
        c.wait_recv()
    across = send_mlp(None, 4, quarter(0), 2, along_x(2))
    x = xr[...].reshape(512, 768)
    square = head_blocks()
    lane = iota((1, 256), 1) // HD
    for j in range(3):
        out = dot(x, wqkv[:, pl.ds(768 * j, 768)]).astype(BF)
        for n in range(3):
            value = out[:, 256 * n : 256 * n + 256]
            if j < 2:
                value = value.astype(F32)
                factor = inverse_norms(value, square)
                if j == 0:
                    row = jnp.zeros((1, 256), F32)
                    for h in range(8):
                        row = jnp.where(lane == h, scale3_ref[8 * n + h], row)
                    factor = factor * row
                value = (value * factor).astype(BF)
            qkv[6 * j + 2 * n] = value[:, :128]
            qkv[6 * j + 2 * n + 1] = value[:, 128:]

    masks = head_masks(4)
    lane = iota((1, 128), 1)
    level = jnp.where(lane < 64, MASK, -MASK).astype(BF)

    def group(g, carry):
        for win in range(2):

            def rows(ref_at):
                return jnp.concatenate(
                    [ref_at(pl.ds(128 * win, 128)), ref_at(pl.ds(256 + 128 * win, 128))], 0
                )

            q, k, v = (rows(lambda r, j=j: qkv[6 * j + g, r, :]) for j in range(3))
            marks = rows(lambda r: aug[r, :])
            keys = jnp.concatenate([k, marks], 1)
            marks = marks * level
            right = jnp.concatenate([v, jnp.ones((256, 128), BF)], 1)
            outs = []
            for h in range(4):
                score = dot_nt(jnp.concatenate([q * masks[h], marks], 1), keys)
                side = [bias3[bias_rows(4 * g + h, t), :] for t in range(3)]
                spot = jnp.concatenate(
                    [
                        jnp.concatenate([side[1], side[2]], 1),
                        jnp.concatenate([side[0], side[1]], 1),
                    ],
                    0,
                )
                outs.append(dot(jnp.exp(score + spot).astype(BF), right))
            out = lane_pick([o[:, :128] for o in outs]) / lane_pick([o[:, 128:] for o in outs])
            out = out.astype(BF)
            cols = pl.ds(pl.multiple_of(g * 128, 128), 128)
            ctx[pl.ds(128 * win, 128), cols] = out[:128]
            ctx[pl.ds(256 + 128 * win, 128), cols] = out[128:]
        return carry

    lax.fori_loop(0, 6, group, 0, unroll=2)

    get_proj3.wait()
    y = dot(ctx[...], wproj[...])
    y = layer_norm(y, gain_attn3[...].reshape(1, 768)) + x.astype(F32)
    y = y.astype(BF).astype(F32)
    for half in range(2):
        for r in range(32):
            source = half * 256 + 8 * r
            for m in range(6):
                bias3[pl.ds(512 * m + r * 16 + half * 8, 8), :] = y[
                    source : source + 8, 128 * m : 128 * m + 128
                ]
    pieces = []
    for j in range(2):
        side = jnp.concatenate(
            [bias3[pl.ds(512 * m + j, 256, stride=2), :] for m in range(6)], 1
        ).reshape(16, 2, 8, 768)
        for i in range(2):
            pieces.append(side[:, i].reshape(128, 768).astype(BF))
    get_merge.wait()
    merged = dot(jnp.concatenate(pieces, 1), wm[...])
    merged = layer_norm(merged, gain_merge[...].reshape(1, 1536)).astype(BF)
    row, col = iota((128, 128), 0), iota((128, 128), 1)
    source = lax.rem(row, 64) // 4 * 8 + row // 64 * 4 + lax.rem(row, 4)
    order = jnp.where(col == source, 1.0, 0.0).astype(BF)
    m4 = part[0]
    m4[...] = dot(order, merged).astype(BF)

    shift = [
        w.go(m4.at[pl.ds(64, 48)], back.at[pl.ds(16, 48)], shifted(0, 1)),
        w.go(m4.at[pl.ds(48, 16)], back.at[pl.ds(64, 16)], shifted(1, 0)),
        w.go(m4.at[pl.ds(112, 16)], back.at[pl.ds(0, 16)], shifted(1, 1)),
    ]
    back[pl.ds(80, 48), :] = m4[pl.ds(0, 48), :]
    for c in flight_t:
        c.wait_recv()

    def build4(n, carry):
        s, h = n // 3, lax.rem(n, 3)
        rows = tabs[s, h]
        tables = bias_tables([rows[m : m + 1] for m in range(4)])
        side = jnp.where(core == 0, tables[2], tables[0])
        for a in range(16):
            bias3[bias_rows(n, 0, 8 * a, 8), :] = bias_block(tables[1], a)
            bias3[bias_rows(n, 1, 8 * a, 8), :] = bias_block(side, a)
        return carry

    lax.fori_loop(0, 12, build4, 0)
    for c in shift:
        c.wait()
    source = lax.rem(row, 8) // 4 * 64 + row // 8 * 4 + lax.rem(row, 4)
    order = jnp.where(col == source, 1.0, 0.0).astype(BF)
    blocks[0] = dot(order, back[...]).astype(BF)
    right = w.go(blocks.at[0], blocks.at[1], along_x(1))
    left = w.go(blocks.at[0], blocks.at[2], along_x(-1))
    crossing = [w.go(blocks.at[0], others.at[0], other_core())]

    late = list(pass_on(piece_a, 768, flight_a) + pass_on(piece_p, 48, flight_p))
    arrive(across)
    spread4 = spread_z(4)
    skew = send_mlp(4, 6, quarter(0), 1, along_y(1))
    skew += send_mlp(4, 6, quarter(0) + 1, 1, along_y(-1))
    mates = send_mlp(4, 5, quarter(0), 2, other_core())
    get_up.wait()
    get_down.wait()
    mates_low = send_mlp(0, 1, 0, 8, other_core())
    beside, spread6, ends = [], [], []

    def attend(b):
        both = jnp.concatenate([blocks[b], others[b]], 0)
        qkv4[...] = dot(both, wa[...]).astype(BF)
        outs = []
        for pair in range(2):
            normed = []
            for n in range(3):
                value = qkv4[:, pl.ds(768 * pair + 256 * n, 256)]
                full = value.astype(F32)
                full = full * inverse_norms(full, square)
                for i in range(2):
                    part_of = slice(128 * i, 128 * i + 128)
                    kind = (2 * n + i) % 3
                    normed.append(value[:, part_of] if kind == 2 else full[:, part_of])
            for s in range(2):
                q, k, v = normed[3 * s : 3 * s + 3]
                q = (q[:128] * tabs[2 * pair + s, 0, pl.ds(4, 1), pl.ds(0, 128)]).astype(BF)
                k = k.astype(BF)
                right = jnp.concatenate([v, jnp.ones((256, 128), BF)], 1)
                sums = []
                for h in range(3):
                    n = 3 * (2 * pair + s) + h
                    spot = jnp.concatenate(
                        [bias3[bias_rows(n, 0), :], bias3[bias_rows(n, 1), :]], 1
                    )
                    score = dot_nt(q * masks[h], k) + spot
                    sums.append(dot(jnp.exp(score).astype(BF), right))
                outs.append(
                    (
                        lane_pick([o[:, :128] for o in sums])
                        / lane_pick([o[:, 128:] for o in sums])
                    ).astype(BF)
                )
        part[b][...] = dot(jnp.concatenate(outs, 1), wp[...].reshape(512, 1536)).astype(BF)

    for flight in (flight_a, flight_p):
        flight[2].wait_recv()
    arrive(late)
    crossing[0].wait_recv()
    attend(0)
    beside += send_mlp(0, 2, 0, 4, along_y(1))
    beside += send_mlp(0, 2, 4, 4, along_y(-1))
    right.wait_recv()
    crossing.append(w.go(blocks.at[1], others.at[1], other_core()))
    on_right = w.go(blocks.at[1, first], blocks.at[3, first], along_x(1))
    left.wait_recv()
    crossing.append(w.go(blocks.at[2], others.at[2], other_core()))
    on_left = w.go(blocks.at[2, second], blocks.at[3, second], along_x(-1))
    crossing[1].wait_recv()
    attend(1)
    sums = [w.go(part[1].at[first], buf4.at[1, first], along_x(-1))]
    arrive(skew)
    spread6 += spread_z(6)
    mates += send_mlp(6, 7, quarter(0), 2, other_core())
    crossing[2].wait_recv()
    attend(2)
    sums.append(w.go(part[2].at[second], buf4.at[0, second], along_x(1)))
    on_right.wait_recv()
    crossing.append(w.go(blocks.at[3, first], others.at[3, first], other_core()))
    on_left.wait_recv()
    crossing.append(w.go(blocks.at[3, second], others.at[3, second], other_core()))
    crossing[3].wait_recv()
    crossing[4].wait_recv()
    attend(3)
    far_right = w.go(part[3].at[first], buf4.at[2, first], along_x(1))
    far_left = w.go(part[3].at[second], buf4.at[2, second], along_x(-1))
    far_right.wait_recv()
    part[2][first, :] = (part[2][first, :].astype(F32) + buf4[2, first, :].astype(F32)).astype(BF)
    sums.append(w.go(part[2].at[first], buf4.at[0, first], along_x(1)))
    far_left.wait_recv()
    part[1][second, :] = (
        part[1][second, :].astype(F32) + buf4[2, second, :].astype(F32)
    ).astype(BF)
    sums.append(w.go(part[1].at[second], buf4.at[1, second], along_x(-1)))
    for slot, flight in ((4, spread4), (6, spread6)):
        onward, copies = forward_z(slot, flight)
        ends.append((slot, onward))
        mates += copies
    arrive(beside)
    mates_low += send_mlp(2, 3, 0, 8, other_core())
    arrive(sums)
    total = part[0][...].astype(F32) + buf4[0].astype(F32) + buf4[1].astype(F32)
    for c in [right, left, on_right, on_left, far_right, far_left] + sums:
        c.wait_send()
    total = layer_norm(total, gain_attn4[...].reshape(1, 1536))
    hidden[...] = (blocks[0].astype(F32) + total).astype(BF)

    visits = [
        w.go(hidden.at[first], visit.at[first], along_x(1)),
        w.go(hidden.at[second], visit.at[second], along_x(-1)),
    ]

    def units(tokens, half):
        return gelu(dot(tokens, wu[:, pl.ds(1536 * half, 1536)])).astype(BF)

    arrive(mates_low)
    own = dot(units(hidden[...], 0), wd[pl.ds(0, 1536), :])
    for slot, copies in ends:
        arrive(copies)
        mates.extend(send_mlp(slot, slot + 1, quarter(2), 2, other_core()))
    arrive(visits)
    guest = dot(units(visit[...], 0), wd[pl.ds(0, 1536), :])
    arrive(mates)
    inner = units(visit[...], 1)
    returns = []
    for n in range(2):
        cols = pl.ds(768 * n, 768)
        value = guest[:, 768 * n : 768 * n + 768] + dot(inner, wd[pl.ds(1536, 1536), cols])
        visit_part[:, cols] = value.astype(BF)
        returns += [
            w.go(visit_part.at[first, cols], bufm.at[first, cols], along_x(-1)),
            w.go(visit_part.at[second, cols], bufm.at[second, cols], along_x(1)),
        ]
    own = own + dot(units(hidden[...], 1), wd[pl.ds(1536, 1536), :])
    sent = halo + flight_t + crossing + late + across + skew + beside + mates + mates_low
    for f in spread4 + tuple(spread6) + flight_a + flight_p:
        sent += f if isinstance(f, list) else [f]
    for slot, copies in ends:
        sent += copies
    for c in sent + visits + returns:
        c.wait_send()
    arrive(returns)
    total = layer_norm(own + bufm[...].astype(F32), gain_mlp4[...].reshape(1, 1536))
    out_ref[...] = (hidden[...].astype(F32) + total).astype(BF).reshape(16, 8, 1536)


def per_device(
    tokens,
    regions,
    w_qkv3,
    w_proj3,
    bias_table3,
    logit_scale3,
    gain_attn3,
    w_merge,
    gain_merge,
    w_qkv4,
    w_proj4,
    bias_table4,
    logit_scale4,
    gain_attn4,
    w_up4,
    w_down4,
    gain_mlp4,
):
    any_ = pl.BlockSpec(memory_space=pl.ANY)
    vm = pl.BlockSpec(memory_space=pltpu.VMEM)
    sm = pl.BlockSpec(memory_space=pltpu.SMEM)
    out = pl.pallas_call(
        whole_kernel,
        name="whole",
        out_shape=jax.ShapeDtypeStruct((16, 8, 1536), BF),
        in_specs=[any_, vm, vm, vm, sm, sm, any_, any_, vm, any_, vm, any_, any_, vm, any_, any_, vm],
        out_specs=vm,
        scratch_shapes=[
            pltpu.VMEM((512, 768), BF),
            pltpu.VMEM((2, 256, 768), BF),
            pltpu.VMEM((2, 256, 768), BF),
            pltpu.VMEM((512, 128), BF),
            pltpu.VMEM((768, 2304), BF),
            pltpu.VMEM((768, 768), BF),
            pltpu.VMEM((3072, 1536), BF),
            pltpu.VMEM((18, 512, 128), BF),
            pltpu.VMEM((72 * 128, 128), F32),
            pltpu.VMEM((4, 3, 8, 256), F32),
            pltpu.VMEM((3, 96, 1536), BF),
            pltpu.VMEM((1536, 1536), BF),
            pltpu.VMEM((4, 128, 1536), BF),
            pltpu.VMEM((4, 128, 1536), BF),
            pltpu.VMEM((4, 128, 1536), BF),
            pltpu.VMEM((3, 128, 1536), BF),
            pltpu.VMEM((128, 1536), BF),
            pltpu.VMEM((1536, 3072), BF),
            pltpu.VMEM((3072, 1536), BF),
            pltpu.SemaphoreType.DMA((WIRES,)),
            pltpu.SemaphoreType.DMA((WIRES,)),
            pltpu.SemaphoreType.DMA((8,)),
        ],
        compiler_params=pltpu.CompilerParams(
            collective_id=1, has_side_effects=True, vmem_limit_bytes=VMEM_LIMIT
        ),
    )(
        tokens.reshape(512, 768),
        regions.T,
        bias_table3.transpose(1, 0, 2),
        bias_table4,
        logit_scale3,
        logit_scale4,
        w_qkv3,
        w_proj3,
        gain_attn3,
        w_merge,
        gain_merge,
        w_qkv4.transpose(0, 2, 1),
        w_proj4,
        gain_attn4,
        w_up4,
        w_down4,
        gain_mlp4,
    )
    return out

def solution(mesh):
    placed = (
        P("wide", "narrow", None),
        P("wide", "narrow"),
        P(),
        P(),
        P(),
        P(),
        P(),
        P(),
        P(),
        P(None, None, "narrow"),
        P("narrow", None),
        P("narrow", None, None),
        P("narrow"),
        P(),
        P(None, "narrow"),
        P("narrow", None),
        P(),
    )
    return jax.shard_map(
        per_device, mesh=mesh, in_specs=placed, out_specs=P("wide", "narrow", None), check_vma=False
    )
```
